128 devices in a mesh: machine: 32 (over x, y, core), local: 4 (over z).
Axes of the slice: x: 4, y: 4, z: 4, core: 2. Of those that a mesh axis runs over, the one named last changes fastest.
Arguments:
- inputs: bfloat16 [32, 1024, 1984], P('machine', 'local'), may hold values from -6 to 6
- out_grads: bfloat16 [32, 1024, 7936], P('machine', 'local'), may hold values from -0.046875 to 0.046875
- error_buf: bfloat16 [32, 1984, 7936], P('machine', 'local'), may hold values from -4 to 4
- q_prev: bfloat16 [7936, 128], replicated, may hold values from -0.0625 to 0.0625
Outputs:
- q_factor: float32 [7936, 128], P('local')
- error_next: bfloat16 [32, 1984, 7936], P('machine', 'local')
The draws below stay inside these ranges and needn't reach their ends.
All inputs are finite; a program needn't handle non-finite values.
Results may differ from the reference program's by a relative error of at most 0.0007.
Values may be sent and summed in bfloat16 or wider, within the bound.
A program may use at most 128 MiB of HBM per device.

```python
import jax
import jax.numpy as jnp
from jax import lax

ROWS = 1984
COLS = 7936
RANK = 128
TOKENS_M = 1024
N_MACHINE = 32


def block_levels(rng, shape, shards, least, high):
    factor_of = 1.0
    for dim, shards_of in shards:
        heights = jax.random.uniform(jax.random.fold_in(jax.random.fold_in(rng, 6), dim), (shards_of,), jnp.float32, least / len(shards), high / len(shards))
        factor_of = factor_of * jnp.repeat(jnp.exp(heights), shape[dim] // shards_of).reshape((-1,) + (1,) * (len(shape) - 1 - dim))
    return factor_of


def gaussian(own_key, dims, width, reach, split=(), held_as=jnp.bfloat16):
    result = width * jax.random.normal(own_key, dims, jnp.float32)
    if split:
        result = result * block_levels(own_key, dims, split, -0.22, 0.18)
    return jnp.clip(result, -reach, reach).astype(held_as)


def setup_inputs(seed: int = 0) -> dict:
    key_of = jax.random.split(jax.random.key(seed), 5)
    inputs = gaussian(key_of[0], (N_MACHINE, TOKENS_M, ROWS), 1.0, 6.0, ((0, 32), (1, 4)))
    out_grads = gaussian(key_of[1], (N_MACHINE, TOKENS_M, COLS), (16 * TOKENS_M) ** -0.5, 0.046875, ((0, 32), (1, 4)))
    error_buf = gaussian(key_of[2], (N_MACHINE, ROWS, COLS), 0.25, 4.0, ((0, 32), (1, 4)))
    q_prev = gaussian(key_of[3], (COLS, RANK), COLS ** -0.5, 0.0625)
    return {"inputs": inputs, "out_grads": out_grads, "error_buf": error_buf, "q_prev": q_prev}


def reference(inputs, out_grads, error_buf, q_prev):
    highest = lax.Precision.HIGHEST

    def form(args):
        xpart, gpart, epart = args
        return jnp.dot(xpart.T.astype(jnp.float32), gpart.astype(jnp.float32), preferred_element_type=jnp.float32) + epart.astype(jnp.float32)
    merged = lax.map(form, (inputs, out_grads, error_buf))
    q_wide = q_prev.astype(jnp.float32)
    p_terms = lax.map(lambda block: jnp.dot(block, q_wide, precision=highest), merged)
    p_mean = jnp.sum(p_terms, axis=0) / N_MACHINE
    gram = jnp.dot(p_mean.T, p_mean, precision=highest)
    chol = jnp.linalg.cholesky(gram)
    p_hat = lax.linalg.triangular_solve(chol, p_mean, left_side=False, lower=True, transpose_a=True)
    q_terms = lax.map(lambda block: jnp.dot(block.T, p_hat, precision=highest), merged)
    q_factor = jnp.sum(q_terms, axis=0) / N_MACHINE
    update = jnp.dot(p_hat, q_factor.T, precision=highest)
    error_next = (merged - update[None]).astype(jnp.bfloat16)
    return (q_factor, error_next)
```

```python
import jax
import jax.numpy as jnp
from jax import lax
from jax.experimental import pallas as pl
from jax.experimental.pallas import tpu as pltpu
from jax.sharding import PartitionSpec as P

MESH = pl.DeviceIdType.MESH
F32, BF16 = jnp.float32, jnp.bfloat16
HIGHEST = lax.Precision.HIGHEST

NX, NY, NC, NZ = 4, 4, 2, 4
TOKENS, ROWS, COLS, RANK = 256, 1984, 7936, 128
MY_ROWS = ROWS // NZ
HALF = TOKENS // 2
CHUNK = 256
CHUNKS = COLS // CHUNK
P_ROWS = 2048
P_SLICE = P_ROWS // 32
PIECES = ((0, 8), (8, 16), (16, 24), (24, 31))
N_PIECE = len(PIECES)
N_COPY = 29


def dot(a, b, lhs=1, rhs=0, precision=None):
    return lax.dot_general(
        a, b, (((lhs,), (rhs,)), ((), ())), precision=precision, preferred_element_type=F32
    )


def split(value):
    high = value.astype(BF16)
    return high, (value - high.astype(F32)).astype(BF16)


def all_reduce(part, from_core, r1x, r1y, r2x, r2y, rz, full, send, recv, place, scale):
    x, y, core, z = place
    height = part.shape[3]
    upper, lower = pl.ds(0, height // 2), pl.ds(height // 2, height // 2)
    running = {}

    def start(key, number, src, dst, where):
        px, py, pcore, pz = where
        copy = pltpu.make_async_remote_copy(
            src_ref=src, dst_ref=dst, send_sem=send.at[number], recv_sem=recv.at[number],
            device_id={"machine": (px * NY + py) * NC + pcore, "local": pz}, device_id_type=MESH,
        )
        copy.start()
        running.setdefault(key, []).append(copy)

    def arrive(key):
        for copy in running[key]:
            copy.wait_recv()

    def begin():
        start("core", 0, part.at[1 - core], from_core, (x, y, 1 - core, z))

    def first():
        arrive("core")

        def add(s, carry):
            a, b = s // NY, s % NY
            part[core, a, b] = part[core, a, b] + from_core[a, b]
            return carry

        lax.fori_loop(0, NX * NY, add, 0)
        for d in range(1, 4):
            px, py = (x + d) % NX, (y + d) % NY
            start("1x", 0 + d, part.at[core, px, :, upper], r1x.at[d - 1], (px, y, core, z))
            start("1y", 3 + d, part.at[core, :, py, lower], r1y.at[d - 1], (x, py, core, z))

    def second():
        arrive("1x")
        arrive("1y")
        for b in range(NY):
            part[core, x, b, upper] = part[core, x, b, upper] + r1x[0, b] + r1x[1, b] + r1x[2, b]
        for a in range(NX):
            part[core, a, y, lower] = part[core, a, y, lower] + r1y[0, a] + r1y[1, a] + r1y[2, a]
        for d in range(1, 4):
            px, py = (x + d) % NX, (y + d) % NY
            start("2y", 6 + d, part.at[core, x, py, upper], r2y.at[d - 1], (x, py, core, z))
            start("2x", 9 + d, part.at[core, px, y, lower], r2x.at[d - 1], (px, y, core, z))

    def across():
        arrive("2x")
        arrive("2y")
        rz[z, upper] = part[core, x, y, upper] + r2y[0] + r2y[1] + r2y[2]
        rz[z, lower] = part[core, x, y, lower] + r2x[0] + r2x[1] + r2x[2]
        for d in range(1, 4):
            start("z", 12 + d, rz.at[z], rz.at[z], (x, y, core, (z + d) % NZ))

    def total():
        arrive("z")
        full[core, x, y] = (rz[0] + rz[1] + rz[2] + rz[3]) * scale
        for d in range(1, 4):
            px, py = (x + d) % NX, (y + d) % NY
            mine = full.at[core, x, y, upper]
            start("3y", 15 + d, mine, mine, (x, py, core, z))
            mine = full.at[core, x, y, lower]
            start("3x", 18 + d, mine, mine, (px, y, core, z))

    def spread():
        arrive("3x")
        arrive("3y")
        for d in range(1, 4):
            px, py = (x + d) % NX, (y + d) % NY
            mine = full.at[core, x, :, upper]
            start("4x", 21 + d, mine, mine, (px, y, core, z))
            mine = full.at[core, :, y, lower]
            start("4y", 24 + d, mine, mine, (x, py, core, z))

    def share():
        arrive("4x")
        arrive("4y")
        start("share", 28, full.at[core], full.at[core], (x, y, 1 - core, z))

    def end():
        arrive("share")

    def sent():
        for copies in running.values():
            for copy in copies:
                copy.wait_send()

    return [begin, first, second, across, total, spread, share, end], sent


def cholesky_inverse(mat):
    lane = lax.broadcasted_iota(jnp.int32, (8, RANK), 1)
    sub = lax.broadcasted_iota(jnp.int32, (8, RANK), 0)

    def panel(b, carry):
        rows = pl.ds(pl.multiple_of(b * 8, 8), 8)
        left = pltpu.roll(mat[rows, 0:RANK], (RANK - b * 8) % RANK, 1)
        right = mat[rows, RANK : 2 * RANK]
        for j in range(8):
            column = jnp.broadcast_to(left[:, j : j + 1], (8, RANK))
            pivot = jnp.broadcast_to(column[j : j + 1, :], (8, RANK))
            inv = lax.rsqrt(pivot)
            inv = inv * (1.5 - 0.5 * pivot * inv * inv)
            row_l = jnp.broadcast_to(left[j : j + 1, :], (8, RANK)) * inv
            row_r = jnp.broadcast_to(right[j : j + 1, :], (8, RANK)) * inv
            factor = column * inv
            left = jnp.where(sub > j, left - factor * row_l, jnp.where(sub == j, row_l, left))
            right = jnp.where(sub > j, right - factor * row_r, jnp.where(sub == j, row_r, right))
        left = pltpu.roll(left, b * 8, 1)
        mat[rows, 0:RANK] = left
        mat[rows, RANK : 2 * RANK] = right
        below = jnp.where(lane >= (b + 1) * 8, left, 0.0)
        both = jnp.concatenate([left, right], axis=1)
        mat[...] = mat[...] - dot(below, both, 0, 0, HIGHEST)
        return carry

    lax.fori_loop(0, RANK // 8, panel, 0)


def kernel(
    xt_hbm, g_hbm, e_hbm, q_hbm, qf_hbm, err_hbm,
    xt, xr, g_all, e_buf, q_in, p_flat, t_acc, mat, p_hat, p_mine, y_cat, p_cat, q_lines,
    p_part, p_core, p1x, p1y, p2x, p2y, p_z, p_full,
    q_part, q_core, q1x, q1y, q2x, q2y, q_z, q_full,
    load, store, p_send, p_recv, q_send, q_recv, x_send, x_recv, g_send, g_recv,
):
    m, z = lax.axis_index("machine"), lax.axis_index("local")
    core, y, x = m % NC, (m // NC) % NY, m // (NC * NY)
    place = (x, y, core, z)
    left, right = (z + NZ - 1) % NZ, (z + 1) % NZ

    loads = [
        pltpu.make_async_copy(g_hbm, g_all.at[pl.ds(z * TOKENS, TOKENS)], load.at[0]),
        pltpu.make_async_copy(q_hbm, q_in, load.at[1]),
        pltpu.make_async_copy(xt_hbm, xt.at[pl.ds(0, ROWS)], load.at[2]),
        pltpu.make_async_copy(e_hbm, e_buf, load.at[3]),
        pltpu.make_async_copy(
            xt_hbm.at[pl.ds(z * MY_ROWS, MY_ROWS)], xr.at[:, pl.ds(z * TOKENS, TOKENS)], load.at[4]
        ),
    ]
    for copy in loads:
        copy.start()

    with jax.named_scope("barrier"):
        barrier = pltpu.get_barrier_semaphore()
        for d in range(1, 4):
            for px, py, pcore, pz in (
                ((x + d) % NX, y, core, z), (x, (y + d) % NY, core, z), (x, y, core, (z + d) % NZ)
            ):
                pl.semaphore_signal(
                    barrier, inc=1, device_id_type=MESH,
                    device_id={"machine": (px * NY + py) * NC + pcore, "local": pz},
                )
        pl.semaphore_signal(
            barrier, inc=1, device_id_type=MESH,
            device_id={"machine": (x * NY + y) * NC + 1 - core, "local": z},
        )
        pl.semaphore_wait(barrier, 10)

    x_copies = []
    for d in range(1, 4):
        pz = (z + d) % NZ
        x_copies.append(pltpu.make_async_remote_copy(
            src_ref=xt_hbm.at[pl.ds(pz * MY_ROWS, MY_ROWS)],
            dst_ref=xr.at[:, pl.ds(z * TOKENS, TOKENS)],
            send_sem=x_send.at[d], recv_sem=x_recv.at[d],
            device_id={"machine": m, "local": pz}, device_id_type=MESH,
        ))
        x_copies[-1].start()

    def g_copy(src, dst, kind, piece, half, owner, target):
        first, last = PIECES[piece]
        rows = pl.ds(owner * TOKENS + half * HALF, HALF)
        cols = pl.ds(first * CHUNK, (last - first) * CHUNK)
        dst = dst.at[rows, cols]
        src = dst if src is None else src.at[pl.ds(half * HALF, HALF), cols]
        return pltpu.make_async_remote_copy(
            src_ref=src, dst_ref=dst, send_sem=g_send.at[kind, piece], recv_sem=g_recv.at[kind, piece],
            device_id={"machine": m, "local": target}, device_id_type=MESH,
        )

    early, late, onward = [], [], []
    for i in range(N_PIECE):
        early += [g_copy(g_hbm, g_all, 0, i, 0, z, right), g_copy(g_hbm, g_all, 1, i, 1, z, left)]
        late += [g_copy(g_hbm, g_all, 2, i, 1, z, right), g_copy(g_hbm, g_all, 3, i, 0, z, left)]
        onward += [g_copy(None, g_all, 4, i, 0, left, right), g_copy(None, g_all, 5, i, 1, right, left)]
    for copy in early:
        copy.start()

    p_steps, p_sent = all_reduce(
        p_part, p_core, p1x, p1y, p2x, p2y, p_z, p_full, p_send, p_recv, place, 1.0 / 32
    )
    q_steps, q_sent = all_reduce(
        q_part, q_core, q1x, q1y, q2x, q2y, q_z, q_full, q_send, q_recv, place, 1.0 / 32
    )

    with jax.named_scope("left_terms"):
        xt[pl.ds(ROWS, P_ROWS - ROWS)] = jnp.zeros((P_ROWS - ROWS, TOKENS), BF16)
        loads[1].wait()
        loads[0].wait()
        t_acc[...] = jnp.zeros_like(t_acc)

        def token_terms(s, carry):
            cols = pl.ds(pl.multiple_of(s * CHUNK, CHUNK), CHUNK)
            t_acc[...] += dot(g_all[pl.ds(pl.multiple_of(z * TOKENS, TOKENS), TOKENS), cols], q_in[cols, :])
            return carry

        lax.fori_loop(0, CHUNKS, token_terms, 0)
        t_high, t_low = split(t_acc[...])
        loads[2].wait()
        p_flat[...] = dot(xt[...], t_high) + dot(xt[...], t_low)
        loads[3].wait()
        mine = pl.ds(pl.multiple_of(z * MY_ROWS, 8), MY_ROWS)

        def error_terms(s, carry):
            cols = pl.ds(pl.multiple_of(s * CHUNK, CHUNK), CHUNK)
            p_flat[mine, :] += dot(e_buf[:, cols], q_in[cols, :])
            return carry

        lax.fori_loop(0, CHUNKS, error_terms, 0)
        p_part[...] = p_flat[...].reshape(p_part.shape)

    with jax.named_scope("left_reduce"):
        for step in p_steps:
            step()

    for copy in late:
        copy.start()

    with jax.named_scope("factor"):
        p_flat[...] = p_full[...].reshape(P_ROWS, RANK)
        mat[:, 0:RANK] = dot(p_flat[...], p_flat[...], 0, 0, HIGHEST)
        diagonal = lax.broadcasted_iota(jnp.int32, (RANK, RANK), 0) == lax.broadcasted_iota(
            jnp.int32, (RANK, RANK), 1
        )
        mat[:, RANK : 2 * RANK] = jnp.where(diagonal, 1.0, 0.0)
    with jax.named_scope("cholesky"):
        cholesky_inverse(mat)

    with jax.named_scope("right_terms"):
        p_hat[...] = dot(p_flat[...], mat[:, RANK : 2 * RANK], 1, 1, HIGHEST)
        high, low = split(p_hat[...])
        y_high, y_low = split(dot(high, xt[...], 0, 0) + dot(low, xt[...], 0, 0))
        y_cat[0:RANK, :] = y_high
        y_cat[RANK : 2 * RANK, :] = y_low
        p_mine[...] = p_hat[mine, :]
        m_high, m_low = split(p_mine[...])
        p_cat[:, 0:RANK] = m_high
        p_cat[:, RANK : 2 * RANK] = m_low
        p_cat[:, 2 * RANK : 3 * RANK] = m_high

        def right_terms(s, carry):
            cols = pl.ds(pl.multiple_of(s * CHUNK, CHUNK), CHUNK)
            g_rows = pl.ds(pl.multiple_of(z * TOKENS, TOKENS), TOKENS)
            both = dot(y_cat[...], g_all[g_rows, cols]) + dot(p_cat[:, 0 : 2 * RANK], e_buf[:, cols], 0, 0)
            q_part[s // 16, (s // 4) % 4, s % 4] = both[0:RANK] + both[RANK : 2 * RANK]
            return carry

        lax.fori_loop(0, CHUNKS, right_terms, 0)
        q_part[1, 3, 3] = jnp.zeros((RANK, CHUNK), F32)

    with jax.named_scope("pass_on"):
        for own, passed in zip(early, onward):
            own.wait_recv()
            passed.start()

    for name, step in zip(
        ("q_begin", "q_first", "q_second", "q_across", "q_total", "q_spread", "q_share", "q_end"), q_steps
    ):
        with jax.named_scope(name):
            step()

    with jax.named_scope("right_factor"):
        first_line = (31 * z) // 4

        def lines(i, carry):
            s = first_line + i
            q_lines[pl.ds(pl.multiple_of(i * CHUNK, CHUNK), CHUNK), :] = q_full[
                s // 16, (s // 4) % 4, s % 4
            ].T
            return carry

        lax.fori_loop(0, 9, lines, 0)
        offset = (CHUNK - 64 * z) % CHUNK
        qf_store = pltpu.make_async_copy(q_lines.at[pl.ds(offset, ROWS)], qf_hbm, store.at[0])
        qf_store.start()

    loads[4].wait()
    for copy in x_copies:
        copy.wait_recv()
    stores = [qf_store]
    for i in range(N_PIECE):
        first, last = PIECES[i]
        with jax.named_scope("error_wait"):
            for copy in late[2 * i : 2 * i + 2] + onward[2 * i : 2 * i + 2]:
                copy.wait_recv()

        def error_chunk(s, carry):
            cols = pl.ds(pl.multiple_of(s * CHUNK, CHUNK), CHUNK)
            q_high, q_low = split(q_full[s // 16, (s // 4) % 4, s % 4])
            merged = dot(xr[...], g_all[:, cols]) + e_buf[:, cols].astype(F32)
            update = dot(p_cat[...], jnp.concatenate([q_high, q_high, q_low], axis=0))
            e_buf[:, cols] = (merged - update).astype(BF16)
            return carry

        with jax.named_scope("error_next"):
            lax.fori_loop(first, last, error_chunk, 0)
        cols = pl.ds(first * CHUNK, (last - first) * CHUNK)
        stores.append(pltpu.make_async_copy(e_buf.at[:, cols], err_hbm.at[:, cols], store.at[1 + i]))
        stores[-1].start()

    with jax.named_scope("finish"):
        p_sent()
        q_sent()
        for copy in x_copies + early + late + onward:
            copy.wait_send()
        for copy in stores:
            copy.wait()


def per_device(inputs, out_grads, error_buf, q_prev):
    any_space = pl.BlockSpec(memory_space=pl.ANY)

    def reduce_scratch(height, width):
        stage = pltpu.VMEM((3, 4, height // 2, width), F32)
        small = pltpu.VMEM((3, height // 2, width), F32)
        return [
            pltpu.VMEM((NC, NX, NY, height, width), F32),
            pltpu.VMEM((NX, NY, height, width), F32),
            stage, stage, small, small,
            pltpu.VMEM((NZ, height, width), F32),
            pltpu.VMEM((NC, NX, NY, height, width), F32),
        ]

    dma = pltpu.SemaphoreType.DMA
    q_factor, error_next = pl.pallas_call(
        kernel,
        out_shape=(
            jax.ShapeDtypeStruct((ROWS, RANK), F32),
            jax.ShapeDtypeStruct((MY_ROWS, COLS), BF16),
        ),
        in_specs=[any_space] * 4,
        out_specs=(any_space, any_space),
        scratch_shapes=[
            pltpu.VMEM((P_ROWS, TOKENS), BF16),
            pltpu.VMEM((MY_ROWS, NZ * TOKENS), BF16),
            pltpu.VMEM((NZ * TOKENS, COLS), BF16),
            pltpu.VMEM((MY_ROWS, COLS), BF16),
            pltpu.VMEM((COLS, RANK), BF16),
            pltpu.VMEM((P_ROWS, RANK), F32),
            pltpu.VMEM((TOKENS, RANK), F32),
            pltpu.VMEM((RANK, 2 * RANK), F32),
            pltpu.VMEM((P_ROWS, RANK), F32),
            pltpu.VMEM((MY_ROWS, RANK), F32),
            pltpu.VMEM((2 * RANK, TOKENS), BF16),
            pltpu.VMEM((MY_ROWS, 3 * RANK), BF16),
            pltpu.VMEM((9 * CHUNK, RANK), F32),
            *reduce_scratch(P_SLICE, RANK),
            *reduce_scratch(RANK, CHUNK),
            dma((5,)), dma((1 + N_PIECE,)),
            dma((N_COPY,)), dma((N_COPY,)), dma((N_COPY,)), dma((N_COPY,)),
            dma((4,)), dma((4,)), dma((6, N_PIECE)), dma((6, N_PIECE)),
        ],
        compiler_params=pltpu.CompilerParams(
            collective_id=0, has_side_effects=True, vmem_limit_bytes=60 * 1024 * 1024
        ),
    )(inputs[0].T, out_grads[0], error_buf[0], q_prev)
    return q_factor, error_next[None]


def solution(mesh):
    in_specs = (
        P("machine", "local", None),
        P("machine", "local", None),
        P("machine", "local", None),
        P(),
    )
    out_specs = (P("local", None), P("machine", "local", None))
    return jax.shard_map(
        per_device, mesh=mesh, in_specs=in_specs, out_specs=out_specs, check_vma=False
    )
```

```python
import jax
import jax.numpy as jnp
from jax import lax
from jax.experimental import pallas as pl
from jax.experimental.pallas import tpu as pltpu
from jax.sharding import PartitionSpec as P

MESH = pl.DeviceIdType.MESH
F32, BF16 = jnp.float32, jnp.bfloat16
HIGHEST = lax.Precision.HIGHEST

NX, NY, NC, NZ = 4, 4, 2, 4
TOKENS, ROWS, COLS, RANK = 256, 1984, 7936, 128
MY_ROWS = ROWS // NZ
HALF = TOKENS // 2
CHUNK = 256
CHUNKS = COLS // CHUNK
P_ROWS = 2048
P_SLICE = P_ROWS // 32
PIECES = ((0, 4), (4, 8), (8, 12), (12, 16), (16, 20), (20, 24), (24, 28), (28, 31))
N_PIECE = len(PIECES)
N_COPY = 29
PANEL = 32
PLAN = {
    "start": (("x", 0, 3), ("early", 0, 2)),
    "p4": (("early", 2, 8), ("late", 0, 4)),
    "q4": (("late", 4, 8), ("onward", 0, 8)),
}


def dot(a, b, lhs=1, rhs=0, precision=None):
    return lax.dot_general(
        a, b, (((lhs,), (rhs,)), ((), ())), precision=precision, preferred_element_type=F32
    )


def split(value):
    high = value.astype(BF16)
    return high, (value - high.astype(F32)).astype(BF16)


def all_reduce(part, from_core, r1x, r1y, r2x, r2y, rz, full, send, recv, place, scale):
    x, y, core, z = place
    height = part.shape[3]
    upper, lower = pl.ds(0, height // 2), pl.ds(height // 2, height // 2)
    running = {}

    def start(key, number, src, dst, where):
        px, py, pcore, pz = where
        copy = pltpu.make_async_remote_copy(
            src_ref=src, dst_ref=dst, send_sem=send.at[number], recv_sem=recv.at[number],
            device_id={"machine": (px * NY + py) * NC + pcore, "local": pz}, device_id_type=MESH,
        )
        copy.start()
        running.setdefault(key, []).append(copy)

    def arrive(key):
        for copy in running[key]:
            copy.wait_recv()

    def begin():
        start("core", 0, part.at[1 - core], from_core, (x, y, 1 - core, z))

    def first():
        arrive("core")

        def add(s, carry):
            a, b = s // NY, s % NY
            part[core, a, b] = part[core, a, b] + from_core[a, b]
            return carry

        lax.fori_loop(0, NX * NY, add, 0)
        for d in range(1, 4):
            px, py = (x + d) % NX, (y + d) % NY
            start("1x", 0 + d, part.at[core, px, :, upper], r1x.at[d - 1], (px, y, core, z))
            start("1y", 3 + d, part.at[core, :, py, lower], r1y.at[d - 1], (x, py, core, z))

    def second():
        arrive("1x")
        arrive("1y")
        for b in range(NY):
            part[core, x, b, upper] = part[core, x, b, upper] + r1x[0, b] + r1x[1, b] + r1x[2, b]
        for a in range(NX):
            part[core, a, y, lower] = part[core, a, y, lower] + r1y[0, a] + r1y[1, a] + r1y[2, a]
        for d in range(1, 4):
            px, py = (x + d) % NX, (y + d) % NY
            start("2y", 6 + d, part.at[core, x, py, upper], r2y.at[d - 1], (x, py, core, z))
            start("2x", 9 + d, part.at[core, px, y, lower], r2x.at[d - 1], (px, y, core, z))

    def across():
        arrive("2x")
        arrive("2y")
        rz[z, upper] = part[core, x, y, upper] + r2y[0] + r2y[1] + r2y[2]
        rz[z, lower] = part[core, x, y, lower] + r2x[0] + r2x[1] + r2x[2]
        for d in range(1, 4):
            start("z", 12 + d, rz.at[z], rz.at[z], (x, y, core, (z + d) % NZ))

    def total():
        arrive("z")
        full[core, x, y] = (rz[0] + rz[1] + rz[2] + rz[3]) * scale
        for d in range(1, 4):
            px, py = (x + d) % NX, (y + d) % NY
            mine = full.at[core, x, y, upper]
            start("3y", 15 + d, mine, mine, (x, py, core, z))
            mine = full.at[core, x, y, lower]
            start("3x", 18 + d, mine, mine, (px, y, core, z))

    def spread():
        arrive("3x")
        arrive("3y")
        for d in range(1, 4):
            px, py = (x + d) % NX, (y + d) % NY
            mine = full.at[core, x, :, upper]
            start("4x", 21 + d, mine, mine, (px, y, core, z))
            mine = full.at[core, :, y, lower]
            start("4y", 24 + d, mine, mine, (x, py, core, z))

    def share():
        arrive("4x")
        arrive("4y")
        start("share", 28, full.at[core], full.at[core], (x, y, 1 - core, z))

    def end():
        arrive("share")

    def sent():
        for copies in running.values():
            for copy in copies:
                copy.wait_send()

    return [begin, first, second, across, total, spread, share, end], sent


def cholesky_inverse(mat):
    shape = (PANEL, RANK)
    lane = lax.broadcasted_iota(jnp.int32, shape, 1)
    sub = lax.broadcasted_iota(jnp.int32, shape, 0)

    def panel(b, carry):
        rows = pl.ds(pl.multiple_of(b * PANEL, PANEL), PANEL)
        left = pltpu.roll(mat[rows, 0:RANK], (RANK - b * PANEL) % RANK, 1)
        right = mat[rows, RANK : 2 * RANK]
        pivots = jnp.ones(shape, F32)
        for first in range(0, PANEL, 8):
            columns = [jnp.broadcast_to(left[:, first + k : first + k + 1], shape) for k in range(8)]
            for k in range(8):
                j = first + k
                pivot = jnp.broadcast_to(columns[k][j : j + 1, :], shape)
                factor = jnp.where(sub > j, columns[k] * (1.0 / pivot), 0.0)
                for n in range(k + 1, 8):
                    columns[n] = columns[n] - factor * columns[n][j : j + 1, :]
                left = left - factor * left[j : j + 1, :]
                right = right - factor * right[j : j + 1, :]
                pivots = jnp.where(sub == j, pivot, pivots)
        scale = lax.rsqrt(pivots)
        scale = scale * (1.5 - 0.5 * pivots * scale * scale)
        left = pltpu.roll(left * scale, b * PANEL, 1)
        right = right * scale
        mat[rows, 0:RANK] = left
        mat[rows, RANK : 2 * RANK] = right
        below = jnp.where(lane >= (b + 1) * PANEL, left, 0.0)
        both = jnp.concatenate([left, right], axis=1)
        mat[...] = mat[...] - dot(below, both, 0, 0, HIGHEST)
        return carry

    lax.fori_loop(0, RANK // PANEL, panel, 0)


def kernel(
    xt_hbm, g_hbm, e_hbm, q_hbm, qf_out, e_buf,
    xt, xr, g_all, q_in, p_flat, t_cat, mat, p_rows, p_t, y_cat, p_cat, q_lines,
    p_part, p_core, p1x, p1y, p2x, p2y, p_z, p_full,
    q_part, q_core, q1x, q1y, q2x, q2y, q_z, q_full,
    load, store, p_send, p_recv, q_send, q_recv, x_send, x_recv, g_send, g_recv,
):
    m, z = lax.axis_index("machine"), lax.axis_index("local")
    core, y, x = m % NC, (m // NC) % NY, m // (NC * NY)
    place = (x, y, core, z)
    left, right = (z + NZ - 1) % NZ, (z + 1) % NZ

    loads = [
        pltpu.make_async_copy(g_hbm, g_all.at[pl.ds(z * TOKENS, TOKENS)], load.at[0]),
        pltpu.make_async_copy(q_hbm, q_in, load.at[1]),
        pltpu.make_async_copy(xt_hbm, xt.at[pl.ds(0, ROWS)], load.at[2]),
        pltpu.make_async_copy(e_hbm, e_buf, load.at[3]),
        pltpu.make_async_copy(
            xt_hbm.at[pl.ds(z * MY_ROWS, MY_ROWS)], xr.at[:, pl.ds(z * TOKENS, TOKENS)], load.at[4]
        ),
    ]
    for copy in loads:
        copy.start()

    with jax.named_scope("barrier"):
        barrier = pltpu.get_barrier_semaphore()
        for d in range(1, 4):
            for px, py, pcore, pz in (
                ((x + d) % NX, y, core, z), (x, (y + d) % NY, core, z), (x, y, core, (z + d) % NZ)
            ):
                pl.semaphore_signal(
                    barrier, inc=1, device_id_type=MESH,
                    device_id={"machine": (px * NY + py) * NC + pcore, "local": pz},
                )
        pl.semaphore_signal(
            barrier, inc=1, device_id_type=MESH,
            device_id={"machine": (x * NY + y) * NC + 1 - core, "local": z},
        )
        pl.semaphore_wait(barrier, 10)

    x_copies = []
    for d in range(1, 4):
        pz = (z + d) % NZ
        x_copies.append(pltpu.make_async_remote_copy(
            src_ref=xt_hbm.at[pl.ds(pz * MY_ROWS, MY_ROWS)],
            dst_ref=xr.at[:, pl.ds(z * TOKENS, TOKENS)],
            send_sem=x_send.at[d], recv_sem=x_recv.at[d],
            device_id={"machine": m, "local": pz}, device_id_type=MESH,
        ))

    def g_copy(src, dst, kind, piece, half, owner, target):
        first, last = PIECES[piece]
        rows = pl.ds(owner * TOKENS + half * HALF, HALF)
        cols = pl.ds(first * CHUNK, (last - first) * CHUNK)
        dst = dst.at[rows, cols]
        src = dst if src is None else src.at[pl.ds(half * HALF, HALF), cols]
        return pltpu.make_async_remote_copy(
            src_ref=src, dst_ref=dst, send_sem=g_send.at[kind, piece], recv_sem=g_recv.at[kind, piece],
            device_id={"machine": m, "local": target}, device_id_type=MESH,
        )

    early, late, onward = [], [], []
    for i in range(N_PIECE):
        early += [g_copy(g_hbm, g_all, 0, i, 0, z, right), g_copy(g_hbm, g_all, 1, i, 1, z, left)]
        late += [g_copy(g_hbm, g_all, 2, i, 1, z, right), g_copy(g_hbm, g_all, 3, i, 0, z, left)]
        onward += [g_copy(None, g_all, 4, i, 0, left, right), g_copy(None, g_all, 5, i, 1, right, left)]
    def due(point):
        for name, first, last in PLAN.get(point, ()):
            for i in range(first, last):
                if name == "x":
                    x_copies[i].start()
                for k in (2 * i, 2 * i + 1):
                    if name == "early":
                        early[k].start()
                    if name == "late":
                        late[k].start()
                    if name == "onward":
                        early[k].wait_recv()
                        onward[k].start()

    due("start")

    p_steps, p_sent = all_reduce(
        p_part, p_core, p1x, p1y, p2x, p2y, p_z, p_full, p_send, p_recv, place, 1.0 / 32
    )
    q_steps, q_sent = all_reduce(
        q_part, q_core, q1x, q1y, q2x, q2y, q_z, q_full, q_send, q_recv, place, 1.0 / 32
    )

    with jax.named_scope("left_terms"):
        xt[pl.ds(ROWS, P_ROWS - ROWS)] = jnp.zeros((P_ROWS - ROWS, TOKENS), BF16)
        loads[1].wait()
        loads[0].wait()
        own = pl.ds(pl.multiple_of(z * TOKENS, TOKENS), TOKENS)
        mine = pl.ds(pl.multiple_of(z * MY_ROWS, 8), MY_ROWS)
        t_cat[...] = jnp.concatenate(
            split(
                dot(g_all[own, 0 : COLS // 2], q_in[0 : COLS // 2, :])
                + dot(g_all[own, COLS // 2 : COLS], q_in[COLS // 2 : COLS, :])
            ),
            axis=1,
        )
        loads[2].wait()
        both = dot(xt[...], t_cat[...])
        p_flat[...] = both[:, 0:RANK] + both[:, RANK : 2 * RANK]
        loads[3].wait()
        p_flat[mine, :] += dot(e_buf[:, 0 : COLS // 2], q_in[0 : COLS // 2, :]) + dot(
            e_buf[:, COLS // 2 : COLS], q_in[COLS // 2 : COLS, :]
        )
        p_part[...] = p_flat[...].reshape(p_part.shape)

    with jax.named_scope("left_reduce"):
        for k, step in enumerate(p_steps):
            due("p%d" % k)
            step()
    due("p8")

    with jax.named_scope("factor"):
        p_flat[...] = p_full[...].reshape(P_ROWS, RANK)
        mat[:, 0:RANK] = dot(p_flat[...], p_flat[...], 0, 0, HIGHEST)
        diagonal = lax.broadcasted_iota(jnp.int32, (RANK, RANK), 0) == lax.broadcasted_iota(
            jnp.int32, (RANK, RANK), 1
        )
        mat[:, RANK : 2 * RANK] = jnp.where(diagonal, 1.0, 0.0)
    with jax.named_scope("cholesky"):
        cholesky_inverse(mat)
    due("chol")

    with jax.named_scope("right_terms"):
        inverse = mat[:, RANK : 2 * RANK]
        p_rows[0:RANK, :], p_rows[RANK : 2 * RANK, :] = split(dot(inverse, p_flat[...], 1, 1, HIGHEST))
        y_sum = dot(p_rows[...], xt[...])
        y_cat[0:RANK, :], y_cat[RANK : 2 * RANK, :] = split(y_sum[0:RANK] + y_sum[RANK : 2 * RANK])
        p_mine = p_flat[mine, :]
        p_t[0:RANK, :], p_t[RANK : 2 * RANK, :] = split(dot(inverse, p_mine, 1, 1, HIGHEST))
        m_high, m_low = split(dot(p_mine, inverse, 1, 1, HIGHEST))
        p_cat[:, 0:RANK] = m_high
        p_cat[:, RANK : 2 * RANK] = m_low
        p_cat[:, 2 * RANK : 3 * RANK] = m_high

        q_part[1, 3, 3] = jnp.zeros((RANK, CHUNK), F32)

        def right_terms(s, carry):
            cols = pl.ds(pl.multiple_of(s * CHUNK, CHUNK), CHUNK)
            both = dot(y_cat[...], g_all[own, cols]) + dot(p_t[...], e_buf[:, cols])
            q_part[s // 16, (s // 4) % 4, s % 4] = both[0:RANK] + both[RANK : 2 * RANK]
            return carry

        other = (1 - core) * 16
        lax.fori_loop(other, other + 15 + core, right_terms, 0)
        due("q0")
        q_steps[0]()
        lax.fori_loop(core * 16, core * 16 + 16 - core, right_terms, 0)

    for k, step in enumerate(q_steps[1:], 1):
        due("q%d" % k)
        step()
    due("q8")

    with jax.named_scope("right_factor"):
        first_line = (31 * z) // 4

        def lines(i, carry):
            s = first_line + i
            q_lines[pl.ds(pl.multiple_of(i * CHUNK, CHUNK), CHUNK), :] = q_full[
                s // 16, (s // 4) % 4, s % 4
            ].T
            return carry

        lax.fori_loop(0, 9, lines, 0)
        offset = (CHUNK - 64 * z) % CHUNK
        qf_store = pltpu.make_async_copy(q_lines.at[pl.ds(offset, ROWS)], qf_out, store.at[0])
        qf_store.start()

    loads[4].wait()
    for copy in x_copies:
        copy.wait_recv()
    stores = [qf_store]
    for i in range(N_PIECE):
        first, last = PIECES[i]
        with jax.named_scope("error_wait"):
            for copy in late[2 * i : 2 * i + 2] + onward[2 * i : 2 * i + 2]:
                copy.wait_recv()

        def error_chunk(s, carry):
            cols = pl.ds(pl.multiple_of(s * CHUNK, CHUNK), CHUNK)
            q_high, q_low = split(q_full[s // 16, (s // 4) % 4, s % 4])
            merged = dot(xr[...], g_all[:, cols]) + e_buf[:, cols].astype(F32)
            update = dot(p_cat[...], jnp.concatenate([q_high, q_high, q_low], axis=0))
            e_buf[:, cols] = (merged - update).astype(BF16)
            return carry

        with jax.named_scope("error_next"):
            lax.fori_loop(first, last, error_chunk, 0)

    with jax.named_scope("finish"):
        p_sent()
        q_sent()
        for copy in x_copies + early + late + onward:
            copy.wait_send()
        for copy in stores:
            copy.wait()


def per_device(inputs, out_grads, error_buf, q_prev):
    any_space = pl.BlockSpec(memory_space=pl.ANY)

    def reduce_scratch(height, width):
        stage = pltpu.VMEM((3, 4, height // 2, width), F32)
        small = pltpu.VMEM((3, height // 2, width), F32)
        return [
            pltpu.VMEM((NC, NX, NY, height, width), F32),
            pltpu.VMEM((NX, NY, height, width), F32),
            stage, stage, small, small,
            pltpu.VMEM((NZ, height, width), F32),
            pltpu.VMEM((NC, NX, NY, height, width), F32),
        ]

    dma = pltpu.SemaphoreType.DMA
    q_factor, error_next = pl.pallas_call(
        kernel,
        out_shape=(
            pltpu.VMEM((ROWS, RANK), F32),
            pltpu.VMEM((MY_ROWS, COLS), BF16),
        ),
        in_specs=[any_space] * 4,
        out_specs=(pl.BlockSpec(memory_space=pltpu.VMEM),) * 2,
        scratch_shapes=[
            pltpu.VMEM((P_ROWS, TOKENS), BF16),
            pltpu.VMEM((MY_ROWS, NZ * TOKENS), BF16),
            pltpu.VMEM((NZ * TOKENS, COLS), BF16),
            pltpu.VMEM((COLS, RANK), BF16),
            pltpu.VMEM((P_ROWS, RANK), F32),
            pltpu.VMEM((TOKENS, 2 * RANK), BF16),
            pltpu.VMEM((RANK, 2 * RANK), F32),
            pltpu.VMEM((2 * RANK, P_ROWS), BF16),
            pltpu.VMEM((2 * RANK, MY_ROWS), BF16),
            pltpu.VMEM((2 * RANK, TOKENS), BF16),
            pltpu.VMEM((MY_ROWS, 3 * RANK), BF16),
            pltpu.VMEM((9 * CHUNK, RANK), F32),
            *reduce_scratch(P_SLICE, RANK),
            *reduce_scratch(RANK, CHUNK),
            dma((5,)), dma((1,)),
            dma((N_COPY,)), dma((N_COPY,)), dma((N_COPY,)), dma((N_COPY,)),
            dma((4,)), dma((4,)), dma((6, N_PIECE)), dma((6, N_PIECE)),
        ],
        compiler_params=pltpu.CompilerParams(
            collective_id=0, has_side_effects=True, vmem_limit_bytes=48 * 1024 * 1024
        ),
    )(inputs[0].T, out_grads[0], error_buf[0], q_prev)
    return q_factor, error_next[None]


def solution(mesh):
    in_specs = (
        P("machine", "local", None),
        P("machine", "local", None),
        P("machine", "local", None),
        P(),
    )
    out_specs = (P("local", None), P("machine", "local", None))
    return jax.shard_map(
        per_device, mesh=mesh, in_specs=in_specs, out_specs=out_specs, check_vma=False
    )
```

```python
import jax
import jax.numpy as jnp
from jax import lax
from jax.experimental import pallas as pl
from jax.experimental.pallas import tpu as pltpu
from jax.sharding import PartitionSpec as P

MESH = pl.DeviceIdType.MESH
F32, BF16 = jnp.float32, jnp.bfloat16
HIGHEST = lax.Precision.HIGHEST

NX, NY, NC, NZ = 4, 4, 2, 4
TOKENS, ROWS, COLS, RANK = 256, 1984, 7936, 128
MY_ROWS = ROWS // NZ
HALF = TOKENS // 2
CHUNK = 256
CHUNKS = COLS // CHUNK
P_ROWS = 2048
P_SLICE = P_ROWS // 32
PIECES = ((0, 5), (5, 10), (10, 15), (15, 20), (20, 24), (24, 28), (28, 30), (30, 31))
N_PIECE = len(PIECES)
N_COPY = 32
PANEL = 32
PLAN = {
    "start": (("x", 0, 3), ("early", 0, 2)),
    "p4": (("early", 6, 8),),
    "p5": (("early", 2, 6), ("late", 0, 4)),
    "q4": (("late", 6, 8),),
    "q5": (("late", 4, 6), ("onward", 0, 8)),
}


def dot(a, b, lhs=1, rhs=0, precision=None):
    return lax.dot_general(
        a, b, (((lhs,), (rhs,)), ((), ())), precision=precision, preferred_element_type=F32
    )


def split(value):
    high = value.astype(BF16)
    return high, (value - high.astype(F32)).astype(BF16)


def all_reduce(part, from_core, r1x, r1y, r2x, r2y, rz, full, send, recv, place, scale):
    x, y, core, z = place
    height = part.shape[3]
    upper, lower = pl.ds(0, height // 2), pl.ds(height // 2, height // 2)
    running = {}

    def quarter(k):
        return pl.ds(pl.multiple_of(k * (height // NZ), 8), height // NZ)

    def start(key, number, src, dst, where):
        px, py, pcore, pz = where
        copy = pltpu.make_async_remote_copy(
            src_ref=src, dst_ref=dst, send_sem=send.at[number], recv_sem=recv.at[number],
            device_id={"machine": (px * NY + py) * NC + pcore, "local": pz}, device_id_type=MESH,
        )
        copy.start()
        running.setdefault(key, []).append(copy)

    def arrive(key):
        for copy in running[key]:
            copy.wait_recv()

    def begin():
        start("core", 0, part.at[1 - core], from_core, (x, y, 1 - core, z))

    def first():
        arrive("core")

        def add(s, carry):
            a, b = s // NY, s % NY
            part[core, a, b] = part[core, a, b] + from_core[a, b]
            return carry

        lax.fori_loop(0, NX * NY, add, 0)
        for d in range(1, 4):
            px, py = (x + d) % NX, (y + d) % NY
            start("1x", 0 + d, part.at[core, px, :, upper], r1x.at[d - 1], (px, y, core, z))
            start("1y", 3 + d, part.at[core, :, py, lower], r1y.at[d - 1], (x, py, core, z))

    def second():
        arrive("1x")
        arrive("1y")
        for b in range(NY):
            part[core, x, b, upper] = part[core, x, b, upper] + r1x[0, b] + r1x[1, b] + r1x[2, b]
        for a in range(NX):
            part[core, a, y, lower] = part[core, a, y, lower] + r1y[0, a] + r1y[1, a] + r1y[2, a]
        for d in range(1, 4):
            px, py = (x + d) % NX, (y + d) % NY
            start("2y", 6 + d, part.at[core, x, py, upper], r2y.at[d - 1], (x, py, core, z))
            start("2x", 9 + d, part.at[core, px, y, lower], r2x.at[d - 1], (px, y, core, z))

    def across():
        arrive("2x")
        arrive("2y")
        part[core, x, y, upper] = part[core, x, y, upper] + r2y[0] + r2y[1] + r2y[2]
        part[core, x, y, lower] = part[core, x, y, lower] + r2x[0] + r2x[1] + r2x[2]
        for d in range(1, 4):
            to = (z + d) % NZ
            start("z", 12 + d, part.at[core, x, y, quarter(to)], rz.at[d - 1], (x, y, core, to))

    def total():
        arrive("z")
        mine = quarter(z)
        full[core, x, y, mine] = (part[core, x, y, mine] + rz[0] + rz[1] + rz[2]) * scale
        for d in range(1, 4):
            mine = full.at[core, x, y, quarter(z)]
            start("zz", 28 + d, mine, mine, (x, y, core, (z + d) % NZ))

    def joined():
        arrive("zz")
        for d in range(1, 4):
            px, py = (x + d) % NX, (y + d) % NY
            mine = full.at[core, x, y, upper]
            start("3y", 15 + d, mine, mine, (x, py, core, z))
            mine = full.at[core, x, y, lower]
            start("3x", 18 + d, mine, mine, (px, y, core, z))

    def spread():
        arrive("3x")
        arrive("3y")
        for d in range(1, 4):
            px, py = (x + d) % NX, (y + d) % NY
            mine = full.at[core, x, :, upper]
            start("4x", 21 + d, mine, mine, (px, y, core, z))
            mine = full.at[core, :, y, lower]
            start("4y", 24 + d, mine, mine, (x, py, core, z))

    def share():
        arrive("4x")
        arrive("4y")
        start("share", 28, full.at[core], full.at[core], (x, y, 1 - core, z))

    def end():
        arrive("share")

    def sent():
        for copies in running.values():
            for copy in copies:
                copy.wait_send()

    return [begin, first, second, across, total, joined, spread, share, end], sent


def cholesky_inverse(mat):
    shape = (PANEL, RANK)
    lane = lax.broadcasted_iota(jnp.int32, shape, 1)
    sub = lax.broadcasted_iota(jnp.int32, shape, 0)

    def panel(b, carry):
        rows = pl.ds(pl.multiple_of(b * PANEL, PANEL), PANEL)
        left = pltpu.roll(mat[rows, 0:RANK], (RANK - b * PANEL) % RANK, 1)
        right = mat[rows, RANK : 2 * RANK]
        pivots = jnp.ones(shape, F32)
        for first in range(0, PANEL, 8):
            columns = [jnp.broadcast_to(left[:, first + k : first + k + 1], shape) for k in range(8)]
            for k in range(8):
                j = first + k
                pivot = jnp.broadcast_to(columns[k][j : j + 1, :], shape)
                factor = jnp.where(sub > j, columns[k] * (1.0 / pivot), 0.0)
                for n in range(k + 1, 8):
                    columns[n] = columns[n] - factor * columns[n][j : j + 1, :]
                left = left - factor * left[j : j + 1, :]
                right = right - factor * right[j : j + 1, :]
                pivots = jnp.where(sub == j, pivot, pivots)
        scale = lax.rsqrt(pivots)
        scale = scale * (1.5 - 0.5 * pivots * scale * scale)
        left = pltpu.roll(left * scale, b * PANEL, 1)
        right = right * scale
        mat[rows, 0:RANK] = left
        mat[rows, RANK : 2 * RANK] = right
        below = jnp.where(lane >= (b + 1) * PANEL, left, 0.0)
        both = jnp.concatenate([left, right], axis=1)
        mat[...] = mat[...] - dot(below, both, 0, 0, HIGHEST)
        return carry

    lax.fori_loop(0, RANK // PANEL, panel, 0)


def kernel(
    xt_hbm, g_hbm, e_hbm, q_hbm, qf_out, e_buf,
    xt, xr, g_all, q_in, p_flat, t_cat, mat, p_rows, p_t, y_cat, p_cat, q_lines,
    p_part, p_core, p1x, p1y, p2x, p2y, p_z, p_full,
    q_part, q_core, q1x, q1y, q2x, q2y, q_z, q_full,
    load, store, p_send, p_recv, q_send, q_recv, x_send, x_recv, g_send, g_recv,
):
    m, z = lax.axis_index("machine"), lax.axis_index("local")
    core, y, x = m % NC, (m // NC) % NY, m // (NC * NY)
    place = (x, y, core, z)
    left, right = (z + NZ - 1) % NZ, (z + 1) % NZ

    loads = [
        pltpu.make_async_copy(g_hbm, g_all.at[pl.ds(z * TOKENS, TOKENS)], load.at[0]),
        pltpu.make_async_copy(q_hbm, q_in, load.at[1]),
        pltpu.make_async_copy(xt_hbm, xt.at[pl.ds(0, ROWS)], load.at[2]),
        pltpu.make_async_copy(e_hbm, e_buf, load.at[3]),
        pltpu.make_async_copy(
            xt_hbm.at[pl.ds(z * MY_ROWS, MY_ROWS)], xr.at[:, pl.ds(z * TOKENS, TOKENS)], load.at[4]
        ),
    ]
    for copy in loads:
        copy.start()

    with jax.named_scope("barrier"):
        barrier = pltpu.get_barrier_semaphore()
        for d in range(1, 4):
            for px, py, pcore, pz in (
                ((x + d) % NX, y, core, z), (x, (y + d) % NY, core, z), (x, y, core, (z + d) % NZ)
            ):
                pl.semaphore_signal(
                    barrier, inc=1, device_id_type=MESH,
                    device_id={"machine": (px * NY + py) * NC + pcore, "local": pz},
                )
        pl.semaphore_signal(
            barrier, inc=1, device_id_type=MESH,
            device_id={"machine": (x * NY + y) * NC + 1 - core, "local": z},
        )
        pl.semaphore_wait(barrier, 10)

    x_copies = []
    for d in range(1, 4):
        pz = (z + d) % NZ
        x_copies.append(pltpu.make_async_remote_copy(
            src_ref=xt_hbm.at[pl.ds(pz * MY_ROWS, MY_ROWS)],
            dst_ref=xr.at[:, pl.ds(z * TOKENS, TOKENS)],
            send_sem=x_send.at[d], recv_sem=x_recv.at[d],
            device_id={"machine": m, "local": pz}, device_id_type=MESH,
        ))

    def g_copy(src, dst, kind, piece, half, owner, target):
        first, last = PIECES[piece]
        rows = pl.ds(owner * TOKENS + half * HALF, HALF)
        cols = pl.ds(first * CHUNK, (last - first) * CHUNK)
        dst = dst.at[rows, cols]
        src = dst if src is None else src.at[pl.ds(half * HALF, HALF), cols]
        return pltpu.make_async_remote_copy(
            src_ref=src, dst_ref=dst, send_sem=g_send.at[kind, piece], recv_sem=g_recv.at[kind, piece],
            device_id={"machine": m, "local": target}, device_id_type=MESH,
        )

    early, late, onward = [], [], []
    for i in range(N_PIECE):
        early += [g_copy(g_hbm, g_all, 0, i, 0, z, right), g_copy(g_hbm, g_all, 1, i, 1, z, left)]
        late += [g_copy(g_hbm, g_all, 2, i, 1, z, right), g_copy(g_hbm, g_all, 3, i, 0, z, left)]
        onward += [g_copy(None, g_all, 4, i, 0, left, right), g_copy(None, g_all, 5, i, 1, right, left)]
    def due(point):
        for name, first, last in PLAN.get(point, ()):
            for i in range(first, last):
                if name == "x":
                    x_copies[i].start()
                for k in (2 * i, 2 * i + 1):
                    if name == "early":
                        early[k].start()
                    if name == "late":
                        late[k].start()
                    if name == "onward":
                        early[k].wait_recv()
                        onward[k].start()

    due("start")

    p_steps, p_sent = all_reduce(
        p_part, p_core, p1x, p1y, p2x, p2y, p_z, p_full, p_send, p_recv, place, 1.0 / 32
    )
    q_steps, q_sent = all_reduce(
        q_part, q_core, q1x, q1y, q2x, q2y, q_z, q_full, q_send, q_recv, place, 1.0 / 32
    )

    with jax.named_scope("left_terms"):
        xt[pl.ds(ROWS, P_ROWS - ROWS)] = jnp.zeros((P_ROWS - ROWS, TOKENS), BF16)
        loads[1].wait()
        loads[0].wait()
        own = pl.ds(pl.multiple_of(z * TOKENS, TOKENS), TOKENS)
        mine = pl.ds(pl.multiple_of(z * MY_ROWS, 8), MY_ROWS)
        t_cat[...] = jnp.concatenate(
            split(
                dot(g_all[own, 0 : COLS // 2], q_in[0 : COLS // 2, :])
                + dot(g_all[own, COLS // 2 : COLS], q_in[COLS // 2 : COLS, :])
            ),
            axis=1,
        )
        loads[2].wait()
        both = dot(xt[...], t_cat[...])
        p_flat[...] = both[:, 0:RANK] + both[:, RANK : 2 * RANK]
        loads[3].wait()
        p_flat[mine, :] += dot(e_buf[:, 0 : COLS // 2], q_in[0 : COLS // 2, :]) + dot(
            e_buf[:, COLS // 2 : COLS], q_in[COLS // 2 : COLS, :]
        )
        p_part[...] = p_flat[...].reshape(p_part.shape)

    with jax.named_scope("left_reduce"):
        for k, step in enumerate(p_steps):
            due("p%d" % k)
            step()

    with jax.named_scope("factor"):
        p_flat[...] = p_full[...].reshape(P_ROWS, RANK)
        mat[:, 0:RANK] = dot(p_flat[...], p_flat[...], 0, 0, HIGHEST)
        diagonal = lax.broadcasted_iota(jnp.int32, (RANK, RANK), 0) == lax.broadcasted_iota(
            jnp.int32, (RANK, RANK), 1
        )
        mat[:, RANK : 2 * RANK] = jnp.where(diagonal, 1.0, 0.0)
    with jax.named_scope("cholesky"):
        cholesky_inverse(mat)

    with jax.named_scope("right_terms"):
        inverse = mat[:, RANK : 2 * RANK]
        p_rows[0:RANK, :], p_rows[RANK : 2 * RANK, :] = split(dot(inverse, p_flat[...], 1, 1, HIGHEST))
        y_sum = dot(p_rows[...], xt[...])
        y_cat[0:RANK, :], y_cat[RANK : 2 * RANK, :] = split(y_sum[0:RANK] + y_sum[RANK : 2 * RANK])
        p_mine = p_flat[mine, :]
        p_t[0:RANK, :], p_t[RANK : 2 * RANK, :] = split(dot(inverse, p_mine, 1, 1, HIGHEST))
        m_high, m_low = split(dot(p_mine, inverse, 1, 1, HIGHEST))
        p_cat[:, 0:RANK] = m_high
        p_cat[:, RANK : 2 * RANK] = m_low
        p_cat[:, 2 * RANK : 3 * RANK] = m_high

        q_part[1, 3, 3] = jnp.zeros((RANK, CHUNK), F32)

        def right_terms(s, carry):
            cols = pl.ds(pl.multiple_of(s * CHUNK, CHUNK), CHUNK)
            both = dot(y_cat[...], g_all[own, cols]) + dot(p_t[...], e_buf[:, cols])
            q_part[s // 16, (s // 4) % 4, s % 4] = both[0:RANK] + both[RANK : 2 * RANK]
            return carry

        other = (1 - core) * 16
        lax.fori_loop(other, other + 15 + core, right_terms, 0)
        due("q0")
        q_steps[0]()
        lax.fori_loop(core * 16, core * 16 + 16 - core, right_terms, 0)

    for k, step in enumerate(q_steps[1:], 1):
        due("q%d" % k)
        step()

    with jax.named_scope("right_factor"):
        first_line = (31 * z) // 4

        def lines(i, carry):
            s = first_line + i
            q_lines[pl.ds(pl.multiple_of(i * CHUNK, CHUNK), CHUNK), :] = q_full[
                s // 16, (s // 4) % 4, s % 4
            ].T
            return carry

        lax.fori_loop(0, 9, lines, 0)
        offset = (CHUNK - 64 * z) % CHUNK
        qf_store = pltpu.make_async_copy(q_lines.at[pl.ds(offset, ROWS)], qf_out, store.at[0])
        qf_store.start()

    loads[4].wait()
    for copy in x_copies:
        copy.wait_recv()
    stores = [qf_store]
    for i in range(N_PIECE):
        first, last = PIECES[i]
        with jax.named_scope("error_wait"):
            for copy in late[2 * i : 2 * i + 2] + onward[2 * i : 2 * i + 2]:
                copy.wait_recv()

        def error_chunk(s, carry):
            cols = pl.ds(pl.multiple_of(s * CHUNK, CHUNK), CHUNK)
            q_high, q_low = split(q_full[s // 16, (s // 4) % 4, s % 4])
            merged = dot(xr[...], g_all[:, cols]) + e_buf[:, cols].astype(F32)
            update = dot(p_cat[...], jnp.concatenate([q_high, q_high, q_low], axis=0))
            e_buf[:, cols] = (merged - update).astype(BF16)
            return carry

        with jax.named_scope("error_next"):
            lax.fori_loop(first, last, error_chunk, 0)

    with jax.named_scope("finish"):
        p_sent()
        q_sent()
        for copy in x_copies + early + late + onward:
            copy.wait_send()
        for copy in stores:
            copy.wait()


def closing(qf_in, err_in, qf_out, err_out, done):
    copies = [pltpu.make_async_copy(qf_in, qf_out, done.at[0])]
    for k, (first, last) in enumerate(((0, 128), (128, 256), (256, 384), (384, MY_ROWS))):
        rows = pl.ds(first, last - first)
        copies.append(pltpu.make_async_copy(err_in.at[rows], err_out.at[0, rows], done.at[1 + k]))
    for copy in copies:
        copy.start()
    for copy in copies:
        copy.wait()


def per_device(inputs, out_grads, error_buf, q_prev):
    any_space = pl.BlockSpec(memory_space=pl.ANY)

    def reduce_scratch(height, width):
        stage = pltpu.VMEM((3, 4, height // 2, width), F32)
        small = pltpu.VMEM((3, height // 2, width), F32)
        return [
            pltpu.VMEM((NC, NX, NY, height, width), F32),
            pltpu.VMEM((NX, NY, height, width), F32),
            stage, stage, small, small,
            pltpu.VMEM((3, height // NZ, width), F32),
            pltpu.VMEM((NC, NX, NY, height, width), F32),
        ]

    dma = pltpu.SemaphoreType.DMA
    q_factor, error_next = pl.pallas_call(
        kernel,
        out_shape=(
            pltpu.VMEM((ROWS, RANK), F32),
            pltpu.VMEM((MY_ROWS, COLS), BF16),
        ),
        in_specs=[any_space] * 4,
        out_specs=(pl.BlockSpec(memory_space=pltpu.VMEM),) * 2,
        scratch_shapes=[
            pltpu.VMEM((P_ROWS, TOKENS), BF16),
            pltpu.VMEM((MY_ROWS, NZ * TOKENS), BF16),
            pltpu.VMEM((NZ * TOKENS, COLS), BF16),
            pltpu.VMEM((COLS, RANK), BF16),
            pltpu.VMEM((P_ROWS, RANK), F32),
            pltpu.VMEM((TOKENS, 2 * RANK), BF16),
            pltpu.VMEM((RANK, 2 * RANK), F32),
            pltpu.VMEM((2 * RANK, P_ROWS), BF16),
            pltpu.VMEM((2 * RANK, MY_ROWS), BF16),
            pltpu.VMEM((2 * RANK, TOKENS), BF16),
            pltpu.VMEM((MY_ROWS, 3 * RANK), BF16),
            pltpu.VMEM((9 * CHUNK, RANK), F32),
            *reduce_scratch(P_SLICE, RANK),
            *reduce_scratch(RANK, CHUNK),
            dma((5,)), dma((1,)),
            dma((N_COPY,)), dma((N_COPY,)), dma((N_COPY,)), dma((N_COPY,)),
            dma((4,)), dma((4,)), dma((6, N_PIECE)), dma((6, N_PIECE)),
        ],
        compiler_params=pltpu.CompilerParams(
            collective_id=0, has_side_effects=True, vmem_limit_bytes=48 * 1024 * 1024
        ),
    )(inputs[0].T, out_grads[0], error_buf[0], q_prev)
    vmem = pl.BlockSpec(memory_space=pltpu.VMEM)
    return pl.pallas_call(
        closing,
        out_shape=(
            jax.ShapeDtypeStruct((ROWS, RANK), F32),
            jax.ShapeDtypeStruct((1, MY_ROWS, COLS), BF16),
        ),
        in_specs=[vmem, vmem],
        out_specs=(any_space, any_space),
        scratch_shapes=[dma((5,))],
        compiler_params=pltpu.CompilerParams(vmem_limit_bytes=1024 * 1024),
    )(*(pltpu.with_memory_space_constraint(v, pltpu.VMEM) for v in (q_factor, error_next)))


def solution(mesh):
    in_specs = (
        P("machine", "local", None),
        P("machine", "local", None),
        P("machine", "local", None),
        P(),
    )
    out_specs = (P("local", None), P("machine", "local", None))
    return jax.shard_map(
        per_device, mesh=mesh, in_specs=in_specs, out_specs=out_specs, check_vma=False
    )
```

```python
import jax
import jax.numpy as jnp
from jax import lax
from jax.experimental import pallas as pl
from jax.experimental.pallas import tpu as pltpu
from jax.sharding import PartitionSpec as P

MESH = pl.DeviceIdType.MESH
F32, BF16 = jnp.float32, jnp.bfloat16
HIGHEST = lax.Precision.HIGHEST

NX, NY, NC, NZ = 4, 4, 2, 4
TOKENS, ROWS, COLS, RANK = 256, 1984, 7936, 128
MY_ROWS = ROWS // NZ
HALF = TOKENS // 2
CHUNK = 256
CHUNKS = COLS // CHUNK
P_ROWS = 2048
P_SLICE = P_ROWS // 32
PIECES = ((0, 5), (5, 10), (10, 15), (15, 20), (20, 24), (24, 28), (28, 30), (30, 31))
N_PIECE = len(PIECES)
TAIL = 28
N_COPY = 32
PANEL = 32
PLAN = {
    "start": (("x", 0, 3), ("early", 0, 2)),
    "p4": (("early", 6, 8),),
    "p5": (("early", 2, 6), ("late", 0, 4)),
    "q4": (("late", 6, 8),),
    "q5": (("late", 4, 6), ("onward", 0, 8)),
}


def dot(a, b, lhs=1, rhs=0, precision=None):
    return lax.dot_general(
        a, b, (((lhs,), (rhs,)), ((), ())), precision=precision, preferred_element_type=F32
    )


def split(value):
    high = value.astype(BF16)
    return high, (value - high.astype(F32)).astype(BF16)


def stacked(q_block):
    high, low = split(q_block)
    return jnp.concatenate([high, high, low], axis=0)


def error_block(xr, g_all, e_buf, p_cat, cols, q_cat):
    merged = dot(xr[...], g_all[:, cols]) + e_buf[:, cols].astype(F32)
    return (merged - dot(p_cat[...], q_cat)).astype(BF16)


def all_reduce(part, from_core, r1x, r1y, r2x, r2y, rz, full, send, recv, place, scale):
    x, y, core, z = place
    height = part.shape[3]
    upper, lower = pl.ds(0, height // 2), pl.ds(height // 2, height // 2)
    running = {}

    def quarter(k):
        return pl.ds(pl.multiple_of(k * (height // NZ), 8), height // NZ)

    def start(key, number, src, dst, where):
        px, py, pcore, pz = where
        copy = pltpu.make_async_remote_copy(
            src_ref=src, dst_ref=dst, send_sem=send.at[number], recv_sem=recv.at[number],
            device_id={"machine": (px * NY + py) * NC + pcore, "local": pz}, device_id_type=MESH,
        )
        copy.start()
        running.setdefault(key, []).append(copy)

    def arrive(key):
        for copy in running[key]:
            copy.wait_recv()

    def begin():
        start("core", 0, part.at[1 - core], from_core, (x, y, 1 - core, z))

    def first():
        arrive("core")

        def add(s, carry):
            a, b = s // NY, s % NY
            part[core, a, b] = part[core, a, b] + from_core[a, b]
            return carry

        lax.fori_loop(0, NX * NY, add, 0)
        for d in range(1, 4):
            px, py = (x + d) % NX, (y + d) % NY
            start("1x", 0 + d, part.at[core, px, :, upper], r1x.at[d - 1], (px, y, core, z))
            start("1y", 3 + d, part.at[core, :, py, lower], r1y.at[d - 1], (x, py, core, z))

    def second():
        arrive("1x")
        arrive("1y")
        for b in range(NY):
            part[core, x, b, upper] = part[core, x, b, upper] + r1x[0, b] + r1x[1, b] + r1x[2, b]
        for a in range(NX):
            part[core, a, y, lower] = part[core, a, y, lower] + r1y[0, a] + r1y[1, a] + r1y[2, a]
        for d in range(1, 4):
            px, py = (x + d) % NX, (y + d) % NY
            start("2y", 6 + d, part.at[core, x, py, upper], r2y.at[d - 1], (x, py, core, z))
            start("2x", 9 + d, part.at[core, px, y, lower], r2x.at[d - 1], (px, y, core, z))

    def across():
        arrive("2x")
        arrive("2y")
        part[core, x, y, upper] = part[core, x, y, upper] + r2y[0] + r2y[1] + r2y[2]
        part[core, x, y, lower] = part[core, x, y, lower] + r2x[0] + r2x[1] + r2x[2]
        for d in range(1, 4):
            to = (z + d) % NZ
            start("z", 12 + d, part.at[core, x, y, quarter(to)], rz.at[d - 1], (x, y, core, to))

    def total():
        arrive("z")
        mine = quarter(z)
        full[core, x, y, mine] = (part[core, x, y, mine] + rz[0] + rz[1] + rz[2]) * scale
        for d in range(1, 4):
            mine = full.at[core, x, y, quarter(z)]
            start("zz", 28 + d, mine, mine, (x, y, core, (z + d) % NZ))

    def joined():
        arrive("zz")
        for d in range(1, 4):
            px, py = (x + d) % NX, (y + d) % NY
            mine = full.at[core, x, y, upper]
            start("3y", 15 + d, mine, mine, (x, py, core, z))
            mine = full.at[core, x, y, lower]
            start("3x", 18 + d, mine, mine, (px, y, core, z))

    def spread():
        arrive("3x")
        arrive("3y")
        for d in range(1, 4):
            px, py = (x + d) % NX, (y + d) % NY
            mine = full.at[core, x, :, upper]
            start("4x", 21 + d, mine, mine, (px, y, core, z))
            mine = full.at[core, :, y, lower]
            start("4y", 24 + d, mine, mine, (x, py, core, z))

    def share():
        arrive("4x")
        arrive("4y")
        start("share", 28, full.at[core], full.at[core], (x, y, 1 - core, z))

    def end():
        arrive("share")

    def sent():
        for copies in running.values():
            for copy in copies:
                copy.wait_send()

    return [begin, first, second, across, total, joined, spread, share, end], sent


def cholesky_inverse(mat):
    shape = (PANEL, RANK)
    lane = lax.broadcasted_iota(jnp.int32, shape, 1)
    sub = lax.broadcasted_iota(jnp.int32, shape, 0)

    def panel(b, carry):
        rows = pl.ds(pl.multiple_of(b * PANEL, PANEL), PANEL)
        left = pltpu.roll(mat[rows, 0:RANK], (RANK - b * PANEL) % RANK, 1)
        right = mat[rows, RANK : 2 * RANK]
        pivots = jnp.ones(shape, F32)
        for first in range(0, PANEL, 8):
            columns = [jnp.broadcast_to(left[:, first + k : first + k + 1], shape) for k in range(8)]
            for k in range(8):
                j = first + k
                pivot = jnp.broadcast_to(columns[k][j : j + 1, :], shape)
                factor = jnp.where(sub > j, columns[k] * (1.0 / pivot), 0.0)
                for n in range(k + 1, 8):
                    columns[n] = columns[n] - factor * columns[n][j : j + 1, :]
                left = left - factor * left[j : j + 1, :]
                right = right - factor * right[j : j + 1, :]
                pivots = jnp.where(sub == j, pivot, pivots)
        scale = lax.rsqrt(pivots)
        scale = scale * (1.5 - 0.5 * pivots * scale * scale)
        left = pltpu.roll(left * scale, b * PANEL, 1)
        right = right * scale
        mat[rows, 0:RANK] = left
        mat[rows, RANK : 2 * RANK] = right
        below = jnp.where(lane >= (b + 1) * PANEL, left, 0.0)
        both = jnp.concatenate([left, right], axis=1)
        mat[...] = mat[...] - dot(below, both, 0, 0, HIGHEST)
        return carry

    lax.fori_loop(0, RANK // PANEL, panel, 0)


def kernel(
    xt_hbm, g_hbm, e_hbm, q_hbm, qf_out, e_buf, xr, g_all, p_cat, q_tail,
    xt, q_in, p_flat, t_cat, mat, p_rows, p_t, y_cat, q_lines,
    p_part, p_core, p1x, p1y, p2x, p2y, p_z, p_full,
    q_part, q_core, q1x, q1y, q2x, q2y, q_z, q_full,
    load, store, p_send, p_recv, q_send, q_recv, x_send, x_recv, g_send, g_recv,
):
    m, z = lax.axis_index("machine"), lax.axis_index("local")
    core, y, x = m % NC, (m // NC) % NY, m // (NC * NY)
    place = (x, y, core, z)
    left, right = (z + NZ - 1) % NZ, (z + 1) % NZ

    loads = [
        pltpu.make_async_copy(g_hbm, g_all.at[pl.ds(z * TOKENS, TOKENS)], load.at[0]),
        pltpu.make_async_copy(q_hbm, q_in, load.at[1]),
        pltpu.make_async_copy(xt_hbm, xt.at[pl.ds(0, ROWS)], load.at[2]),
        pltpu.make_async_copy(e_hbm, e_buf, load.at[3]),
        pltpu.make_async_copy(
            xt_hbm.at[pl.ds(z * MY_ROWS, MY_ROWS)], xr.at[:, pl.ds(z * TOKENS, TOKENS)], load.at[4]
        ),
    ]
    for copy in loads:
        copy.start()

    with jax.named_scope("barrier"):
        barrier = pltpu.get_barrier_semaphore()
        for d in range(1, 4):
            for px, py, pcore, pz in (
                ((x + d) % NX, y, core, z), (x, (y + d) % NY, core, z), (x, y, core, (z + d) % NZ)
            ):
                pl.semaphore_signal(
                    barrier, inc=1, device_id_type=MESH,
                    device_id={"machine": (px * NY + py) * NC + pcore, "local": pz},
                )
        pl.semaphore_signal(
            barrier, inc=1, device_id_type=MESH,
            device_id={"machine": (x * NY + y) * NC + 1 - core, "local": z},
        )
        pl.semaphore_wait(barrier, 10)

    x_copies = []
    for d in range(1, 4):
        pz = (z + d) % NZ
        x_copies.append(pltpu.make_async_remote_copy(
            src_ref=xt_hbm.at[pl.ds(pz * MY_ROWS, MY_ROWS)],
            dst_ref=xr.at[:, pl.ds(z * TOKENS, TOKENS)],
            send_sem=x_send.at[d], recv_sem=x_recv.at[d],
            device_id={"machine": m, "local": pz}, device_id_type=MESH,
        ))

    def g_copy(src, dst, kind, piece, half, owner, target):
        first, last = PIECES[piece]
        rows = pl.ds(owner * TOKENS + half * HALF, HALF)
        cols = pl.ds(first * CHUNK, (last - first) * CHUNK)
        dst = dst.at[rows, cols]
        src = dst if src is None else src.at[pl.ds(half * HALF, HALF), cols]
        return pltpu.make_async_remote_copy(
            src_ref=src, dst_ref=dst, send_sem=g_send.at[kind, piece], recv_sem=g_recv.at[kind, piece],
            device_id={"machine": m, "local": target}, device_id_type=MESH,
        )

    early, late, onward = [], [], []
    for i in range(N_PIECE):
        early += [g_copy(g_hbm, g_all, 0, i, 0, z, right), g_copy(g_hbm, g_all, 1, i, 1, z, left)]
        late += [g_copy(g_hbm, g_all, 2, i, 1, z, right), g_copy(g_hbm, g_all, 3, i, 0, z, left)]
        onward += [g_copy(None, g_all, 4, i, 0, left, right), g_copy(None, g_all, 5, i, 1, right, left)]
    def due(point):
        for name, first, last in PLAN.get(point, ()):
            for i in range(first, last):
                if name == "x":
                    x_copies[i].start()
                for k in (2 * i, 2 * i + 1):
                    if name == "early":
                        early[k].start()
                    if name == "late":
                        late[k].start()
                    if name == "onward":
                        early[k].wait_recv()
                        onward[k].start()

    due("start")

    p_steps, p_sent = all_reduce(
        p_part, p_core, p1x, p1y, p2x, p2y, p_z, p_full, p_send, p_recv, place, 1.0 / 32
    )
    q_steps, q_sent = all_reduce(
        q_part, q_core, q1x, q1y, q2x, q2y, q_z, q_full, q_send, q_recv, place, 1.0 / 32
    )

    with jax.named_scope("left_terms"):
        xt[pl.ds(ROWS, P_ROWS - ROWS)] = jnp.zeros((P_ROWS - ROWS, TOKENS), BF16)
        loads[1].wait()
        loads[0].wait()
        own = pl.ds(pl.multiple_of(z * TOKENS, TOKENS), TOKENS)
        mine = pl.ds(pl.multiple_of(z * MY_ROWS, 8), MY_ROWS)
        t_cat[...] = jnp.concatenate(
            split(
                dot(g_all[own, 0 : COLS // 2], q_in[0 : COLS // 2, :])
                + dot(g_all[own, COLS // 2 : COLS], q_in[COLS // 2 : COLS, :])
            ),
            axis=1,
        )
        loads[2].wait()
        both = dot(xt[...], t_cat[...])
        p_flat[...] = both[:, 0:RANK] + both[:, RANK : 2 * RANK]
        loads[3].wait()
        p_flat[mine, :] += dot(e_buf[:, 0 : COLS // 2], q_in[0 : COLS // 2, :]) + dot(
            e_buf[:, COLS // 2 : COLS], q_in[COLS // 2 : COLS, :]
        )
        p_part[...] = p_flat[...].reshape(p_part.shape)

    with jax.named_scope("left_reduce"):
        for k, step in enumerate(p_steps):
            due("p%d" % k)
            step()

    with jax.named_scope("factor"):
        p_flat[...] = p_full[...].reshape(P_ROWS, RANK)
        mat[:, 0:RANK] = dot(p_flat[...], p_flat[...], 0, 0, HIGHEST)
        diagonal = lax.broadcasted_iota(jnp.int32, (RANK, RANK), 0) == lax.broadcasted_iota(
            jnp.int32, (RANK, RANK), 1
        )
        mat[:, RANK : 2 * RANK] = jnp.where(diagonal, 1.0, 0.0)
    with jax.named_scope("cholesky"):
        cholesky_inverse(mat)

    with jax.named_scope("right_terms"):
        inverse = mat[:, RANK : 2 * RANK]
        p_rows[0:RANK, :], p_rows[RANK : 2 * RANK, :] = split(dot(inverse, p_flat[...], 1, 1, HIGHEST))
        y_sum = dot(p_rows[...], xt[...])
        y_cat[0:RANK, :], y_cat[RANK : 2 * RANK, :] = split(y_sum[0:RANK] + y_sum[RANK : 2 * RANK])
        p_mine = p_flat[mine, :]
        p_t[0:RANK, :], p_t[RANK : 2 * RANK, :] = split(dot(inverse, p_mine, 1, 1, HIGHEST))
        m_high, m_low = split(dot(p_mine, inverse, 1, 1, HIGHEST))
        p_cat[:, 0:RANK] = m_high
        p_cat[:, RANK : 2 * RANK] = m_low
        p_cat[:, 2 * RANK : 3 * RANK] = m_high

        q_part[1, 3, 3] = jnp.zeros((RANK, CHUNK), F32)

        def right_terms(s, carry):
            cols = pl.ds(pl.multiple_of(s * CHUNK, CHUNK), CHUNK)
            both = dot(y_cat[...], g_all[own, cols]) + dot(p_t[...], e_buf[:, cols])
            q_part[s // 16, (s // 4) % 4, s % 4] = both[0:RANK] + both[RANK : 2 * RANK]
            return carry

        other = (1 - core) * 16
        lax.fori_loop(other, other + 15 + core, right_terms, 0)
        due("q0")
        q_steps[0]()
        lax.fori_loop(core * 16, core * 16 + 16 - core, right_terms, 0)

    for k, step in enumerate(q_steps[1:], 1):
        due("q%d" % k)
        step()

    with jax.named_scope("right_factor"):
        first_line = (31 * z) // 4

        def lines(i, carry):
            s = first_line + i
            q_lines[pl.ds(pl.multiple_of(i * CHUNK, CHUNK), CHUNK), :] = q_full[
                s // 16, (s // 4) % 4, s % 4
            ].T
            return carry

        lax.fori_loop(0, 9, lines, 0)
        offset = (CHUNK - 64 * z) % CHUNK
        qf_store = pltpu.make_async_copy(q_lines.at[pl.ds(offset, ROWS)], qf_out, store.at[0])
        qf_store.start()

    for s in range(TAIL, CHUNKS):
        q_tail[s - TAIL] = stacked(q_full[s // 16, (s // 4) % 4, s % 4])
    loads[4].wait()
    for copy in x_copies:
        copy.wait_recv()
    stores = [qf_store]
    for i in range(N_PIECE):
        first, last = PIECES[i]
        with jax.named_scope("error_wait"):
            for copy in late[2 * i : 2 * i + 2] + onward[2 * i : 2 * i + 2]:
                copy.wait_recv()

        def error_chunk(s, carry):
            cols = pl.ds(pl.multiple_of(s * CHUNK, CHUNK), CHUNK)
            q_cat = stacked(q_full[s // 16, (s // 4) % 4, s % 4])
            e_buf[:, cols] = error_block(xr, g_all, e_buf, p_cat, cols, q_cat)
            return carry

        if last <= TAIL:
            with jax.named_scope("error_next"):
                lax.fori_loop(first, last, error_chunk, 0)

    with jax.named_scope("finish"):
        p_sent()
        q_sent()
        for copy in x_copies + early + late + onward:
            copy.wait_send()
        for copy in stores:
            copy.wait()


def closing(qf_in, e_buf, xr, g_all, p_cat, q_tail, qf_out, err_out, tail, done):
    copies = [pltpu.make_async_copy(qf_in, qf_out, done.at[0])]
    for k in range(4):
        cols = pl.ds(k * TAIL // 4 * CHUNK, TAIL // 4 * CHUNK)
        copies.append(pltpu.make_async_copy(e_buf.at[:, cols], err_out.at[0, :, cols], done.at[1 + k]))
    for copy in copies:
        copy.start()
    for i in range(CHUNKS - TAIL):
        cols = pl.ds((TAIL + i) * CHUNK, CHUNK)
        tail[i] = error_block(xr, g_all, e_buf, p_cat, cols, q_tail[i])
        copies.append(pltpu.make_async_copy(tail.at[i], err_out.at[0, :, cols], done.at[5 + i]))
        copies[-1].start()
    for copy in copies:
        copy.wait()


def per_device(inputs, out_grads, error_buf, q_prev):
    any_space = pl.BlockSpec(memory_space=pl.ANY)
    vmem = pl.BlockSpec(memory_space=pltpu.VMEM)

    def reduce_scratch(height, width):
        stage = pltpu.VMEM((3, 4, height // 2, width), F32)
        small = pltpu.VMEM((3, height // 2, width), F32)
        return [
            pltpu.VMEM((NC, NX, NY, height, width), F32),
            pltpu.VMEM((NX, NY, height, width), F32),
            stage, stage, small, small,
            pltpu.VMEM((3, height // NZ, width), F32),
            pltpu.VMEM((NC, NX, NY, height, width), F32),
        ]

    dma = pltpu.SemaphoreType.DMA
    held = pl.pallas_call(
        kernel,
        out_shape=(
            pltpu.VMEM((ROWS, RANK), F32),
            pltpu.VMEM((MY_ROWS, COLS), BF16),
            pltpu.VMEM((MY_ROWS, NZ * TOKENS), BF16),
            pltpu.VMEM((NZ * TOKENS, COLS), BF16),
            pltpu.VMEM((MY_ROWS, 3 * RANK), BF16),
            pltpu.VMEM((CHUNKS - TAIL, 3 * RANK, CHUNK), BF16),
        ),
        in_specs=[any_space] * 4,
        out_specs=(vmem,) * 6,
        scratch_shapes=[
            pltpu.VMEM((P_ROWS, TOKENS), BF16),
            pltpu.VMEM((COLS, RANK), BF16),
            pltpu.VMEM((P_ROWS, RANK), F32),
            pltpu.VMEM((TOKENS, 2 * RANK), BF16),
            pltpu.VMEM((RANK, 2 * RANK), F32),
            pltpu.VMEM((2 * RANK, P_ROWS), BF16),
            pltpu.VMEM((2 * RANK, MY_ROWS), BF16),
            pltpu.VMEM((2 * RANK, TOKENS), BF16),
            pltpu.VMEM((9 * CHUNK, RANK), F32),
            *reduce_scratch(P_SLICE, RANK),
            *reduce_scratch(RANK, CHUNK),
            dma((5,)), dma((1,)),
            dma((N_COPY,)), dma((N_COPY,)), dma((N_COPY,)), dma((N_COPY,)),
            dma((4,)), dma((4,)), dma((6, N_PIECE)), dma((6, N_PIECE)),
        ],
        compiler_params=pltpu.CompilerParams(
            collective_id=0, has_side_effects=True, vmem_limit_bytes=32 * 1024 * 1024
        ),
    )(inputs[0].T, out_grads[0], error_buf[0], q_prev)
    return pl.pallas_call(
        closing,
        out_shape=(
            jax.ShapeDtypeStruct((ROWS, RANK), F32),
            jax.ShapeDtypeStruct((1, MY_ROWS, COLS), BF16),
        ),
        in_specs=[vmem] * 6,
        out_specs=(any_space, any_space),
        scratch_shapes=[
            pltpu.VMEM((CHUNKS - TAIL, MY_ROWS, CHUNK), BF16),
            dma((5 + CHUNKS - TAIL,)),
        ],
        compiler_params=pltpu.CompilerParams(vmem_limit_bytes=6 * 1024 * 1024),
    )(*(pltpu.with_memory_space_constraint(v, pltpu.VMEM) for v in held))


def solution(mesh):
    in_specs = (
        P("machine", "local", None),
        P("machine", "local", None),
        P("machine", "local", None),
        P(),
    )
    out_specs = (P("local", None), P("machine", "local", None))
    return jax.shard_map(
        per_device, mesh=mesh, in_specs=in_specs, out_specs=out_specs, check_vma=False
    )
```

```python
import jax
import jax.numpy as jnp
from jax import lax
from jax.experimental import pallas as pl
from jax.experimental.pallas import tpu as pltpu
from jax.sharding import PartitionSpec as P

MESH = pl.DeviceIdType.MESH
F32, BF16 = jnp.float32, jnp.bfloat16
HIGHEST = lax.Precision.HIGHEST

NX, NY, NC, NZ = 4, 4, 2, 4
TOKENS, ROWS, COLS, RANK = 256, 1984, 7936, 128
MY_ROWS = ROWS // NZ
HALF = TOKENS // 2
CHUNK = 256
CHUNKS = COLS // CHUNK
P_ROWS = 2048
P_SLICE = P_ROWS // 32
PIECES = ((0, 5), (5, 10), (10, 15), (15, 20), (20, 24), (24, 28), (28, 30), (30, 31))
N_PIECE = len(PIECES)
TAIL = 28
N_COPY = 34
PANEL = 32
PLAN = {
    "start": (("x", 0, 3), ("early", 0, 2)),
    "p4": (("early", 6, 8),),
    "p5": (("early", 2, 6), ("late", 0, 4)),
    "q4": (("late", 6, 7),),
    "q5": (("late", 4, 5),),
    "q6": (("late", 5, 6),),
    "q7": (("late", 7, 8), ("onward", 0, 8)),
}


def dot(a, b, lhs=1, rhs=0, precision=None):
    return lax.dot_general(
        a, b, (((lhs,), (rhs,)), ((), ())), precision=precision, preferred_element_type=F32
    )


def split(value):
    high = value.astype(BF16)
    return high, (value - high.astype(F32)).astype(BF16)


def slot(s):
    return s % NC, s // (NC * NY), s // NC % NY


def stacked(q_block):
    high, low = split(q_block)
    return jnp.concatenate([high, high, low], axis=0)


def error_block(xr, g_all, e_buf, p_cat, cols, q_cat):
    merged = dot(xr[...], g_all[:, cols]) + e_buf[:, cols].astype(F32)
    return (merged - dot(p_cat[...], q_cat)).astype(BF16)


def all_reduce(part, from_core, r1x, r1y, r2x, r2y, rz_half, rz, full, send, recv, place, scale, relayed):
    x, y, core, z = place
    height = part.shape[3]
    upper, lower = pl.ds(0, height // 2), pl.ds(height // 2, height // 2)
    running = {}

    up, across_z, down = (z + 1) % NZ, (z + 2) % NZ, (z + 3) % NZ

    def quarter(k):
        return pl.ds(pl.multiple_of(k * (height // NZ), 8), height // NZ)

    def half(k, which):
        size = height // NZ // 2
        return pl.ds(pl.multiple_of(k * 2 * size + which * size, 8), size)

    def start(key, number, src, dst, where):
        px, py, pcore, pz = where
        copy = pltpu.make_async_remote_copy(
            src_ref=src, dst_ref=dst, send_sem=send.at[number], recv_sem=recv.at[number],
            device_id={"machine": (px * NY + py) * NC + pcore, "local": pz}, device_id_type=MESH,
        )
        copy.start()
        running.setdefault(key, []).append(copy)

    def arrive(key):
        for copy in running[key]:
            copy.wait_recv()

    def begin():
        start("core", 0, part.at[1 - core], from_core, (x, y, 1 - core, z))

    def first():
        arrive("core")

        def add(s, carry):
            a, b = s // NY, s % NY
            part[core, a, b] = part[core, a, b] + from_core[a, b]
            return carry

        lax.fori_loop(0, NX * NY, add, 0)
        for d in range(1, 4):
            px, py = (x + d) % NX, (y + d) % NY
            start("1x", 0 + d, part.at[core, px, :, upper], r1x.at[d - 1], (px, y, core, z))
            start("1y", 3 + d, part.at[core, :, py, lower], r1y.at[d - 1], (x, py, core, z))

    def second():
        arrive("1x")
        arrive("1y")
        for b in range(NY):
            part[core, x, b, upper] = part[core, x, b, upper] + r1x[0, b] + r1x[1, b] + r1x[2, b]
        for a in range(NX):
            part[core, a, y, lower] = part[core, a, y, lower] + r1y[0, a] + r1y[1, a] + r1y[2, a]
        for d in range(1, 4):
            px, py = (x + d) % NX, (y + d) % NY
            start("2y", 6 + d, part.at[core, x, py, upper], r2y.at[d - 1], (x, py, core, z))
            start("2x", 9 + d, part.at[core, px, y, lower], r2x.at[d - 1], (px, y, core, z))

    def across():
        arrive("2x")
        arrive("2y")
        part[core, x, y, upper] = part[core, x, y, upper] + r2y[0] + r2y[1] + r2y[2]
        part[core, x, y, lower] = part[core, x, y, lower] + r2x[0] + r2x[1] + r2x[2]
        mine = part.at[core, x, y]
        if not relayed:
            for d in range(1, 4):
                to = (z + d) % NZ
                start("zb", 12 + d, mine.at[quarter(to)], rz.at[d - 1], (x, y, core, to))
            return
        start("za", 13, mine.at[half(across_z, 0)], rz_half.at[0], (x, y, core, up))
        start("za", 14, mine.at[half(across_z, 1)], rz_half.at[1], (x, y, core, down))

    def relay():
        arrive("za")
        part[core, x, y, half(up, 0)] = part[core, x, y, half(up, 0)] + rz_half[0]
        part[core, x, y, half(down, 1)] = part[core, x, y, half(down, 1)] + rz_half[1]
        mine = part.at[core, x, y]
        start("zb", 15, mine.at[quarter(up)], rz.at[0], (x, y, core, up))
        start("zb", 29, mine.at[quarter(down)], rz.at[1], (x, y, core, down))

    def total():
        arrive("zb")
        mine = quarter(z)
        others = rz[0] + rz[1] if relayed else rz[0] + rz[1] + rz[2]
        full[core, x, y, mine] = (part[core, x, y, mine] + others) * scale
        mine = full.at[core, x, y, quarter(z)]
        if not relayed:
            for d in range(1, 4):
                start("zd", 28 + d, mine, mine, (x, y, core, (z + d) % NZ))
            return
        start("zc", 30, mine, mine, (x, y, core, up))
        start("zc", 31, mine, mine, (x, y, core, down))

    def onward():
        arrive("zc")
        mine = full.at[core, x, y, half(down, 0)]
        start("zd", 32, mine, mine, (x, y, core, up))
        mine = full.at[core, x, y, half(up, 1)]
        start("zd", 33, mine, mine, (x, y, core, down))

    def joined():
        arrive("zd")
        for d in range(1, 4):
            px, py = (x + d) % NX, (y + d) % NY
            mine = full.at[core, x, y, upper]
            start("3y", 15 + d, mine, mine, (x, py, core, z))
            mine = full.at[core, x, y, lower]
            start("3x", 18 + d, mine, mine, (px, y, core, z))

    def spread():
        arrive("3x")
        arrive("3y")
        for d in range(1, 4):
            px, py = (x + d) % NX, (y + d) % NY
            mine = full.at[core, x, :, upper]
            start("4x", 21 + d, mine, mine, (px, y, core, z))
            mine = full.at[core, :, y, lower]
            start("4y", 24 + d, mine, mine, (x, py, core, z))

    def share():
        arrive("4x")
        arrive("4y")
        start("share", 28, full.at[core], full.at[core], (x, y, 1 - core, z))

    def end():
        arrive("share")

    def sent():
        for copies in running.values():
            for copy in copies:
                copy.wait_send()

    if relayed:
        return [begin, first, second, across, relay, total, onward, joined, spread, share, end], sent
    return [begin, first, second, across, total, joined, spread, share, end], sent


def cholesky_inverse(mat):
    shape = (PANEL, RANK)
    lane = lax.broadcasted_iota(jnp.int32, shape, 1)
    sub = lax.broadcasted_iota(jnp.int32, shape, 0)

    def panel(b, carry):
        rows = pl.ds(pl.multiple_of(b * PANEL, PANEL), PANEL)
        left = pltpu.roll(mat[rows, 0:RANK], (RANK - b * PANEL) % RANK, 1)
        right = mat[rows, RANK : 2 * RANK]
        pivots = jnp.ones(shape, F32)
        for first in range(0, PANEL, 8):
            columns = [jnp.broadcast_to(left[:, first + k : first + k + 1], shape) for k in range(8)]
            for k in range(8):
                j = first + k
                pivot = jnp.broadcast_to(columns[k][j : j + 1, :], shape)
                factor = jnp.where(sub > j, columns[k] * (1.0 / pivot), 0.0)
                for n in range(k + 1, 8):
                    columns[n] = columns[n] - factor * columns[n][j : j + 1, :]
                left = left - factor * left[j : j + 1, :]
                right = right - factor * right[j : j + 1, :]
                pivots = jnp.where(sub == j, pivot, pivots)
        scale = lax.rsqrt(pivots)
        scale = scale * (1.5 - 0.5 * pivots * scale * scale)
        left = pltpu.roll(left * scale, b * PANEL, 1)
        right = right * scale
        mat[rows, 0:RANK] = left
        mat[rows, RANK : 2 * RANK] = right
        below = jnp.where(lane >= (b + 1) * PANEL, left, 0.0)
        both = jnp.concatenate([left, right], axis=1)
        mat[...] = mat[...] - dot(below, both, 0, 0, HIGHEST)
        return carry

    lax.fori_loop(0, RANK // PANEL, panel, 0)


def kernel(
    xt_hbm, g_hbm, e_hbm, q_hbm, qf_out, e_buf, xr, g_all, p_cat, q_tail,
    xt, q_in, p_flat, t_cat, mat, p_rows, p_t, y_cat, q_lines,
    p_part, p_core, p1x, p1y, p2x, p2y, p_zh, p_z, p_full,
    q_part, q_core, q1x, q1y, q2x, q2y, q_zh, q_z, q_full,
    load, store, p_send, p_recv, q_send, q_recv, x_send, x_recv, g_send, g_recv,
):
    m, z = lax.axis_index("machine"), lax.axis_index("local")
    core, y, x = m % NC, (m // NC) % NY, m // (NC * NY)
    place = (x, y, core, z)
    left, right = (z + NZ - 1) % NZ, (z + 1) % NZ

    with jax.named_scope("barrier"):
        barrier = pltpu.get_barrier_semaphore()
        for d in range(1, 4):
            for px, py, pcore, pz in (
                (x, y, core, (z + d) % NZ), ((x + d) % NX, y, core, z), (x, (y + d) % NY, core, z)
            ):
                pl.semaphore_signal(
                    barrier, inc=1, device_id_type=MESH,
                    device_id={"machine": (px * NY + py) * NC + pcore, "local": pz},
                )
        pl.semaphore_signal(
            barrier, inc=1, device_id_type=MESH,
            device_id={"machine": (x * NY + y) * NC + 1 - core, "local": z},
        )

    loads = [
        pltpu.make_async_copy(g_hbm, g_all.at[pl.ds(z * TOKENS, TOKENS)], load.at[0]),
        pltpu.make_async_copy(q_hbm, q_in, load.at[1]),
        pltpu.make_async_copy(xt_hbm, xt.at[pl.ds(0, ROWS)], load.at[2]),
        pltpu.make_async_copy(e_hbm, e_buf, load.at[3]),
        pltpu.make_async_copy(
            xt_hbm.at[pl.ds(z * MY_ROWS, MY_ROWS)], xr.at[:, pl.ds(z * TOKENS, TOKENS)], load.at[4]
        ),
    ]
    for copy in loads:
        copy.start()

    pl.semaphore_wait(barrier, 10)

    x_copies = []
    for d in range(1, 4):
        pz = (z + d) % NZ
        x_copies.append(pltpu.make_async_remote_copy(
            src_ref=xt_hbm.at[pl.ds(pz * MY_ROWS, MY_ROWS)],
            dst_ref=xr.at[:, pl.ds(z * TOKENS, TOKENS)],
            send_sem=x_send.at[d], recv_sem=x_recv.at[d],
            device_id={"machine": m, "local": pz}, device_id_type=MESH,
        ))

    def g_copy(src, dst, kind, piece, half, owner, target):
        first, last = PIECES[piece]
        rows = pl.ds(owner * TOKENS + half * HALF, HALF)
        cols = pl.ds(first * CHUNK, (last - first) * CHUNK)
        dst = dst.at[rows, cols]
        src = dst if src is None else src.at[pl.ds(half * HALF, HALF), cols]
        return pltpu.make_async_remote_copy(
            src_ref=src, dst_ref=dst, send_sem=g_send.at[kind, piece], recv_sem=g_recv.at[kind, piece],
            device_id={"machine": m, "local": target}, device_id_type=MESH,
        )

    early, late, onward = [], [], []
    for i in range(N_PIECE):
        early += [g_copy(g_hbm, g_all, 0, i, 0, z, right), g_copy(g_hbm, g_all, 1, i, 1, z, left)]
        late += [g_copy(g_hbm, g_all, 2, i, 1, z, right), g_copy(g_hbm, g_all, 3, i, 0, z, left)]
        onward += [g_copy(None, g_all, 4, i, 0, left, right), g_copy(None, g_all, 5, i, 1, right, left)]
    def due(point):
        for name, first, last in PLAN.get(point, ()):
            for i in range(first, last):
                if name == "x":
                    x_copies[i].start()
                for k in (2 * i, 2 * i + 1):
                    if name == "early":
                        early[k].start()
                    if name == "late":
                        late[k].start()
                    if name == "onward":
                        early[k].wait_recv()
                        onward[k].start()

    due("start")

    p_steps, p_sent = all_reduce(
        p_part, p_core, p1x, p1y, p2x, p2y, p_zh, p_z, p_full, p_send, p_recv, place, 1.0 / 32, False
    )
    q_steps, q_sent = all_reduce(
        q_part, q_core, q1x, q1y, q2x, q2y, q_zh, q_z, q_full, q_send, q_recv, place, 1.0 / 32, True
    )

    with jax.named_scope("left_terms"):
        xt[pl.ds(ROWS, P_ROWS - ROWS)] = jnp.zeros((P_ROWS - ROWS, TOKENS), BF16)
        loads[1].wait()
        loads[0].wait()
        own = pl.ds(pl.multiple_of(z * TOKENS, TOKENS), TOKENS)
        mine = pl.ds(pl.multiple_of(z * MY_ROWS, 8), MY_ROWS)
        t_cat[...] = jnp.concatenate(
            split(
                dot(g_all[own, 0 : COLS // 2], q_in[0 : COLS // 2, :])
                + dot(g_all[own, COLS // 2 : COLS], q_in[COLS // 2 : COLS, :])
            ),
            axis=1,
        )
        loads[2].wait()
        both = dot(xt[...], t_cat[...])
        p_flat[...] = both[:, 0:RANK] + both[:, RANK : 2 * RANK]
        loads[3].wait()
        p_flat[mine, :] += dot(e_buf[:, 0 : COLS // 2], q_in[0 : COLS // 2, :]) + dot(
            e_buf[:, COLS // 2 : COLS], q_in[COLS // 2 : COLS, :]
        )
        p_part[...] = p_flat[...].reshape(p_part.shape)

    with jax.named_scope("left_reduce"):
        for k, step in enumerate(p_steps):
            due("p%d" % k)
            step()

    with jax.named_scope("factor"):
        p_flat[...] = p_full[...].reshape(P_ROWS, RANK)
        mat[:, 0:RANK] = dot(p_flat[...], p_flat[...], 0, 0, HIGHEST)
        diagonal = lax.broadcasted_iota(jnp.int32, (RANK, RANK), 0) == lax.broadcasted_iota(
            jnp.int32, (RANK, RANK), 1
        )
        mat[:, RANK : 2 * RANK] = jnp.where(diagonal, 1.0, 0.0)
    with jax.named_scope("cholesky"):
        cholesky_inverse(mat)

    with jax.named_scope("right_terms"):
        inverse = mat[:, RANK : 2 * RANK]
        p_rows[0:RANK, :], p_rows[RANK : 2 * RANK, :] = split(dot(inverse, p_flat[...], 1, 1, HIGHEST))
        y_sum = dot(p_rows[...], xt[...])
        y_cat[0:RANK, :], y_cat[RANK : 2 * RANK, :] = split(y_sum[0:RANK] + y_sum[RANK : 2 * RANK])
        p_mine = p_flat[mine, :]
        p_t[0:RANK, :], p_t[RANK : 2 * RANK, :] = split(dot(inverse, p_mine, 1, 1, HIGHEST))
        m_high, m_low = split(dot(p_mine, inverse, 1, 1, HIGHEST))
        p_cat[:, 0:RANK] = m_high
        p_cat[:, RANK : 2 * RANK] = m_low
        p_cat[:, 2 * RANK : 3 * RANK] = m_high

        q_part[1, 3, 3] = jnp.zeros((RANK, CHUNK), F32)

        def right_terms(which):
            def chunk(i, carry):
                s = NC * i + which
                cols = pl.ds(pl.multiple_of(s * CHUNK, CHUNK), CHUNK)
                both = dot(y_cat[...], g_all[own, cols]) + dot(p_t[...], e_buf[:, cols])
                q_part[slot(s)] = both[0:RANK] + both[RANK : 2 * RANK]
                return carry

            lax.fori_loop(0, 16 - which, chunk, 0)

        right_terms(1 - core)
        due("q0")
        q_steps[0]()
        right_terms(core)

    for k, step in enumerate(q_steps[1:-1], 1):
        due("q%d" % k)
        step()

    loads[4].wait()
    for copy in x_copies:
        copy.wait_recv()

    def wait_piece(i):
        for copy in late[2 * i : 2 * i + 2] + onward[2 * i : 2 * i + 2]:
            copy.wait_recv()

    def error_chunk(s, carry):
        cols = pl.ds(pl.multiple_of(s * CHUNK, CHUNK), CHUNK)
        e_buf[:, cols] = error_block(xr, g_all, e_buf, p_cat, cols, stacked(q_full[slot(s)]))
        return carry

    with jax.named_scope("error_next"):
        wait_piece(0)
        wait_piece(1)
        ahead = PIECES[1][1] // NC
        lax.fori_loop(0, ahead, lambda i, carry: error_chunk(NC * i + core, carry), 0)
        q_steps[-1]()
        lax.fori_loop(0, ahead, lambda i, carry: error_chunk(NC * i + 1 - core, carry), 0)
        for i in range(2, N_PIECE - 3):
            wait_piece(i)
            lax.fori_loop(*PIECES[i], error_chunk, 0)

    with jax.named_scope("right_factor"):
        first_line = (31 * z) // 4

        def lines(i, carry):
            s = first_line + i
            q_lines[pl.ds(pl.multiple_of(i * CHUNK, CHUNK), CHUNK), :] = q_full[slot(s)].T
            return carry

        lax.fori_loop(0, 9, lines, 0)
        offset = (CHUNK - 64 * z) % CHUNK
        qf_store = pltpu.make_async_copy(q_lines.at[pl.ds(offset, ROWS)], qf_out, store.at[0])
        qf_store.start()
        for s in range(TAIL, CHUNKS):
            q_tail[s - TAIL] = stacked(q_full[slot(s)])

    with jax.named_scope("error_next_end"):
        wait_piece(N_PIECE - 3)
        lax.fori_loop(*PIECES[N_PIECE - 3], error_chunk, 0)
        wait_piece(N_PIECE - 2)
        wait_piece(N_PIECE - 1)

    with jax.named_scope("finish"):
        p_sent()
        q_sent()
        for copy in x_copies + early + late + onward:
            copy.wait_send()
        qf_store.wait()


def closing(qf_in, e_buf, xr, g_all, p_cat, q_tail, qf_out, err_out, tail, done):
    copies = [pltpu.make_async_copy(qf_in, qf_out, done.at[0])]
    for k in range(4):
        cols = pl.ds(k * TAIL // 4 * CHUNK, TAIL // 4 * CHUNK)
        copies.append(pltpu.make_async_copy(e_buf.at[:, cols], err_out.at[0, :, cols], done.at[1 + k]))
    for copy in copies:
        copy.start()
    for i in range(CHUNKS - TAIL):
        cols = pl.ds((TAIL + i) * CHUNK, CHUNK)
        tail[i] = error_block(xr, g_all, e_buf, p_cat, cols, q_tail[i])
        copies.append(pltpu.make_async_copy(tail.at[i], err_out.at[0, :, cols], done.at[5 + i]))
        copies[-1].start()
    for copy in copies:
        copy.wait()


def per_device(inputs, out_grads, error_buf, q_prev):
    any_space = pl.BlockSpec(memory_space=pl.ANY)
    vmem = pl.BlockSpec(memory_space=pltpu.VMEM)

    def reduce_scratch(height, width):
        stage = pltpu.VMEM((3, 4, height // 2, width), F32)
        small = pltpu.VMEM((3, height // 2, width), F32)
        return [
            pltpu.VMEM((NC, NX, NY, height, width), F32),
            pltpu.VMEM((NX, NY, height, width), F32),
            stage, stage, small, small,
            pltpu.VMEM((2, height // NZ // 2, width), F32),
            pltpu.VMEM((3, height // NZ, width), F32),
            pltpu.VMEM((NC, NX, NY, height, width), F32),
        ]

    dma = pltpu.SemaphoreType.DMA
    held = pl.pallas_call(
        kernel,
        out_shape=(
            pltpu.VMEM((ROWS, RANK), F32),
            pltpu.VMEM((MY_ROWS, COLS), BF16),
            pltpu.VMEM((MY_ROWS, NZ * TOKENS), BF16),
            pltpu.VMEM((NZ * TOKENS, COLS), BF16),
            pltpu.VMEM((MY_ROWS, 3 * RANK), BF16),
            pltpu.VMEM((CHUNKS - TAIL, 3 * RANK, CHUNK), BF16),
        ),
        in_specs=[any_space] * 4,
        out_specs=(vmem,) * 6,
        scratch_shapes=[
            pltpu.VMEM((P_ROWS, TOKENS), BF16),
            pltpu.VMEM((COLS, RANK), BF16),
            pltpu.VMEM((P_ROWS, RANK), F32),
            pltpu.VMEM((TOKENS, 2 * RANK), BF16),
            pltpu.VMEM((RANK, 2 * RANK), F32),
            pltpu.VMEM((2 * RANK, P_ROWS), BF16),
            pltpu.VMEM((2 * RANK, MY_ROWS), BF16),
            pltpu.VMEM((2 * RANK, TOKENS), BF16),
            pltpu.VMEM((9 * CHUNK, RANK), F32),
            *reduce_scratch(P_SLICE, RANK),
            *reduce_scratch(RANK, CHUNK),
            dma((5,)), dma((1,)),
            dma((N_COPY,)), dma((N_COPY,)), dma((N_COPY,)), dma((N_COPY,)),
            dma((4,)), dma((4,)), dma((6, N_PIECE)), dma((6, N_PIECE)),
        ],
        compiler_params=pltpu.CompilerParams(
            collective_id=0, has_side_effects=True, vmem_limit_bytes=32 * 1024 * 1024
        ),
    )(inputs[0].T, out_grads[0], error_buf[0], q_prev)
    return pl.pallas_call(
        closing,
        out_shape=(
            jax.ShapeDtypeStruct((ROWS, RANK), F32),
            jax.ShapeDtypeStruct((1, MY_ROWS, COLS), BF16),
        ),
        in_specs=[vmem] * 6,
        out_specs=(any_space, any_space),
        scratch_shapes=[
            pltpu.VMEM((CHUNKS - TAIL, MY_ROWS, CHUNK), BF16),
            dma((5 + CHUNKS - TAIL,)),
        ],
        compiler_params=pltpu.CompilerParams(vmem_limit_bytes=6 * 1024 * 1024),
    )(*(pltpu.with_memory_space_constraint(v, pltpu.VMEM) for v in held))


def solution(mesh):
    in_specs = (
        P("machine", "local", None),
        P("machine", "local", None),
        P("machine", "local", None),
        P(),
    )
    out_specs = (P("local", None), P("machine", "local", None))
    return jax.shard_map(
        per_device, mesh=mesh, in_specs=in_specs, out_specs=out_specs, check_vma=False
    )
```

```python
import jax
import jax.numpy as jnp
from jax import lax
from jax.experimental import pallas as pl
from jax.experimental.pallas import tpu as pltpu
from jax.sharding import PartitionSpec as P

MESH = pl.DeviceIdType.MESH
F32, BF16 = jnp.float32, jnp.bfloat16
HIGHEST = lax.Precision.HIGHEST

NX, NY, NC, NZ = 4, 4, 2, 4
TOKENS, ROWS, COLS, RANK = 256, 1984, 7936, 128
MY_ROWS = ROWS // NZ
HALF = TOKENS // 2
CHUNK = 256
CHUNKS = COLS // CHUNK
P_ROWS = 2048
P_SLICE = P_ROWS // 32
PIECES = ((0, 5), (5, 10), (10, 15), (15, 20), (20, 24), (24, 28), (28, 30), (30, 31))
N_PIECE = len(PIECES)
TAIL = 28
N_COPY = 34
PANEL = 32
PLAN = {
    "start": (("x", 0, 3), ("early", 0, 2)),
    "p4": (("early", 6, 8),),
    "p5": (("early", 2, 6), ("late", 0, 4)),
    "q4": (("late", 6, 7),),
    "q5": (("late", 4, 5),),
    "q6": (("late", 5, 6),),
    "q7": (("late", 7, 8), ("onward", 0, 8)),
}


def dot(a, b, lhs=1, rhs=0, precision=None):
    return lax.dot_general(
        a, b, (((lhs,), (rhs,)), ((), ())), precision=precision, preferred_element_type=F32
    )


def split(value):
    high = value.astype(BF16)
    return high, (value - high.astype(F32)).astype(BF16)


def slot(s):
    return s % NC, s // (NC * NY), s // NC % NY


def stacked(q_block):
    high, low = split(q_block)
    return jnp.concatenate([high, high, low], axis=0)


def error_block(xr, g_all, e_buf, p_cat, cols, q_cat):
    merged = dot(xr[...], g_all[:, cols]) + e_buf[:, cols].astype(F32)
    return (merged - dot(p_cat[...], q_cat)).astype(BF16)


def all_reduce(part, from_core, r1x, r1y, r2x, r2y, rz_half, rz, full, send, recv, place, scale, relayed):
    x, y, core, z = place
    height = part.shape[3]
    upper, lower = pl.ds(0, height // 2), pl.ds(height // 2, height // 2)
    running = {}

    up, across_z, down = (z + 1) % NZ, (z + 2) % NZ, (z + 3) % NZ

    def quarter(k):
        return pl.ds(pl.multiple_of(k * (height // NZ), 8), height // NZ)

    def half(k, which):
        size = height // NZ // 2
        return pl.ds(pl.multiple_of(k * 2 * size + which * size, 8), size)

    def start(key, number, src, dst, where):
        px, py, pcore, pz = where
        copy = pltpu.make_async_remote_copy(
            src_ref=src, dst_ref=dst, send_sem=send.at[number], recv_sem=recv.at[number],
            device_id={"machine": (px * NY + py) * NC + pcore, "local": pz}, device_id_type=MESH,
        )
        copy.start()
        running.setdefault(key, []).append(copy)

    def arrive(key):
        for copy in running[key]:
            copy.wait_recv()

    def begin():
        start("core", 0, part.at[1 - core], from_core, (x, y, 1 - core, z))

    def first():
        arrive("core")

        def add(s, carry):
            a, b = s // NY, s % NY
            part[core, a, b] = part[core, a, b] + from_core[a, b]
            return carry

        lax.fori_loop(0, NX * NY, add, 0)
        for d in range(1, 4):
            px, py = (x + d) % NX, (y + d) % NY
            start("1x", 0 + d, part.at[core, px, :, upper], r1x.at[d - 1], (px, y, core, z))
            start("1y", 3 + d, part.at[core, :, py, lower], r1y.at[d - 1], (x, py, core, z))

    def second():
        arrive("1x")
        arrive("1y")
        for b in range(NY):
            part[core, x, b, upper] = part[core, x, b, upper] + r1x[0, b] + r1x[1, b] + r1x[2, b]
        for a in range(NX):
            part[core, a, y, lower] = part[core, a, y, lower] + r1y[0, a] + r1y[1, a] + r1y[2, a]
        for d in range(1, 4):
            px, py = (x + d) % NX, (y + d) % NY
            start("2y", 6 + d, part.at[core, x, py, upper], r2y.at[d - 1], (x, py, core, z))
            start("2x", 9 + d, part.at[core, px, y, lower], r2x.at[d - 1], (px, y, core, z))

    def across():
        arrive("2x")
        arrive("2y")
        part[core, x, y, upper] = part[core, x, y, upper] + r2y[0] + r2y[1] + r2y[2]
        part[core, x, y, lower] = part[core, x, y, lower] + r2x[0] + r2x[1] + r2x[2]
        mine = part.at[core, x, y]
        if not relayed:
            for d in range(1, 4):
                to = (z + d) % NZ
                start("zb", 12 + d, mine.at[quarter(to)], rz.at[d - 1], (x, y, core, to))
            return
        start("za", 13, mine.at[half(across_z, 0)], rz_half.at[0], (x, y, core, up))
        start("za", 14, mine.at[half(across_z, 1)], rz_half.at[1], (x, y, core, down))

    def relay():
        arrive("za")
        part[core, x, y, half(up, 0)] = part[core, x, y, half(up, 0)] + rz_half[0]
        part[core, x, y, half(down, 1)] = part[core, x, y, half(down, 1)] + rz_half[1]
        mine = part.at[core, x, y]
        start("zb", 15, mine.at[quarter(up)], rz.at[0], (x, y, core, up))
        start("zb", 29, mine.at[quarter(down)], rz.at[1], (x, y, core, down))

    def total():
        arrive("zb")
        mine = quarter(z)
        others = rz[0] + rz[1] if relayed else rz[0] + rz[1] + rz[2]
        full[core, x, y, mine] = (part[core, x, y, mine] + others) * scale
        mine = full.at[core, x, y, quarter(z)]
        if not relayed:
            for d in range(1, 4):
                start("zd", 28 + d, mine, mine, (x, y, core, (z + d) % NZ))
            return
        start("zc", 30, mine, mine, (x, y, core, up))
        start("zc", 31, mine, mine, (x, y, core, down))

    def onward():
        arrive("zc")
        mine = full.at[core, x, y, half(down, 0)]
        start("zd", 32, mine, mine, (x, y, core, up))
        mine = full.at[core, x, y, half(up, 1)]
        start("zd", 33, mine, mine, (x, y, core, down))

    def joined():
        arrive("zd")
        for d in range(1, 4):
            px, py = (x + d) % NX, (y + d) % NY
            mine = full.at[core, x, y, upper]
            start("3y", 15 + d, mine, mine, (x, py, core, z))
            mine = full.at[core, x, y, lower]
            start("3x", 18 + d, mine, mine, (px, y, core, z))

    def spread():
        arrive("3x")
        arrive("3y")
        for d in range(1, 4):
            px, py = (x + d) % NX, (y + d) % NY
            mine = full.at[core, x, :, upper]
            start("4x", 21 + d, mine, mine, (px, y, core, z))
            mine = full.at[core, :, y, lower]
            start("4y", 24 + d, mine, mine, (x, py, core, z))

    def share():
        arrive("4x")
        arrive("4y")
        start("share", 28, full.at[core], full.at[core], (x, y, 1 - core, z))

    def end():
        arrive("share")

    def sent():
        for copies in running.values():
            for copy in copies:
                copy.wait_send()

    if relayed:
        return [begin, first, second, across, relay, total, onward, joined, spread, share, end], sent
    return [begin, first, second, across, total, joined, spread, share, end], sent


def cholesky_inverse(mat):
    shape = (PANEL, RANK)
    lane = lax.broadcasted_iota(jnp.int32, shape, 1)
    sub = lax.broadcasted_iota(jnp.int32, shape, 0)

    def panel(b, carry):
        rows = pl.ds(pl.multiple_of(b * PANEL, PANEL), PANEL)
        left = pltpu.roll(mat[rows, 0:RANK], (RANK - b * PANEL) % RANK, 1)
        right = mat[rows, RANK : 2 * RANK]
        pivots = jnp.ones(shape, F32)
        for first in range(0, PANEL, 8):
            columns = [jnp.broadcast_to(left[:, first + k : first + k + 1], shape) for k in range(8)]
            for k in range(8):
                j = first + k
                pivot = jnp.broadcast_to(columns[k][j : j + 1, :], shape)
                factor = jnp.where(sub > j, columns[k] * (1.0 / pivot), 0.0)
                for n in range(k + 1, 8):
                    columns[n] = columns[n] - factor * columns[n][j : j + 1, :]
                left = left - factor * left[j : j + 1, :]
                right = right - factor * right[j : j + 1, :]
                pivots = jnp.where(sub == j, pivot, pivots)
        scale = lax.rsqrt(pivots)
        scale = scale * (1.5 - 0.5 * pivots * scale * scale)
        left = pltpu.roll(left * scale, b * PANEL, 1)
        right = right * scale
        mat[rows, 0:RANK] = left
        mat[rows, RANK : 2 * RANK] = right
        below = jnp.where(lane >= (b + 1) * PANEL, left, 0.0)
        both = jnp.concatenate([left, right], axis=1)
        mat[...] = mat[...] - dot(below, both, 0, 0, HIGHEST)
        return carry

    lax.fori_loop(0, RANK // PANEL, panel, 0)


def kernel(
    xt_hbm, g_hbm, e_hbm, q_hbm, qf_out, e_buf, xr, g_all, p_cat, q_tail,
    xt, q_in, p_flat, t_cat, mat, p_rows, p_t, y_cat, q_lines,
    p_part, p_core, p1x, p1y, p2x, p2y, p_zh, p_z, p_full,
    q_part, q_core, q1x, q1y, q2x, q2y, q_zh, q_z, q_full,
    load, store, p_send, p_recv, q_send, q_recv, x_send, x_recv, g_send, g_recv,
):
    m, z = lax.axis_index("machine"), lax.axis_index("local")
    core, y, x = m % NC, (m // NC) % NY, m // (NC * NY)
    place = (x, y, core, z)
    left, right = (z + NZ - 1) % NZ, (z + 1) % NZ

    with jax.named_scope("barrier"):
        barrier = pltpu.get_barrier_semaphore()
        for d in range(1, 4):
            for px, py, pcore, pz in (
                (x, y, core, (z + d) % NZ), ((x + d) % NX, y, core, z), (x, (y + d) % NY, core, z)
            ):
                pl.semaphore_signal(
                    barrier, inc=1, device_id_type=MESH,
                    device_id={"machine": (px * NY + py) * NC + pcore, "local": pz},
                )
        pl.semaphore_signal(
            barrier, inc=1, device_id_type=MESH,
            device_id={"machine": (x * NY + y) * NC + 1 - core, "local": z},
        )

    loads = [
        pltpu.make_async_copy(g_hbm, g_all.at[pl.ds(z * TOKENS, TOKENS)], load.at[0]),
        pltpu.make_async_copy(q_hbm, q_in, load.at[1]),
        pltpu.make_async_copy(xt_hbm, xt.at[pl.ds(0, ROWS)], load.at[2]),
        pltpu.make_async_copy(e_hbm, e_buf, load.at[3]),
        pltpu.make_async_copy(
            xt_hbm.at[pl.ds(z * MY_ROWS, MY_ROWS)], xr.at[:, pl.ds(z * TOKENS, TOKENS)], load.at[4]
        ),
    ]
    for copy in loads:
        copy.start()

    pl.semaphore_wait(barrier, 10)

    x_copies = []
    for d in range(1, 4):
        pz = (z + d) % NZ
        x_copies.append(pltpu.make_async_remote_copy(
            src_ref=xt_hbm.at[pl.ds(pz * MY_ROWS, MY_ROWS)],
            dst_ref=xr.at[:, pl.ds(z * TOKENS, TOKENS)],
            send_sem=x_send.at[d], recv_sem=x_recv.at[d],
            device_id={"machine": m, "local": pz}, device_id_type=MESH,
        ))

    def g_copy(src, dst, kind, piece, half, owner, target):
        first, last = PIECES[piece]
        rows = pl.ds(owner * TOKENS + half * HALF, HALF)
        cols = pl.ds(first * CHUNK, (last - first) * CHUNK)
        dst = dst.at[rows, cols]
        src = dst if src is None else src.at[pl.ds(half * HALF, HALF), cols]
        return pltpu.make_async_remote_copy(
            src_ref=src, dst_ref=dst, send_sem=g_send.at[kind, piece], recv_sem=g_recv.at[kind, piece],
            device_id={"machine": m, "local": target}, device_id_type=MESH,
        )

    early, late, onward = [], [], []
    for i in range(N_PIECE):
        early += [g_copy(g_hbm, g_all, 0, i, 0, z, right), g_copy(g_hbm, g_all, 1, i, 1, z, left)]
        late += [g_copy(g_hbm, g_all, 2, i, 1, z, right), g_copy(g_hbm, g_all, 3, i, 0, z, left)]
        onward += [g_copy(None, g_all, 4, i, 0, left, right), g_copy(None, g_all, 5, i, 1, right, left)]
    def due(point):
        for name, first, last in PLAN.get(point, ()):
            for i in range(first, last):
                if name == "x":
                    x_copies[i].start()
                for k in (2 * i, 2 * i + 1):
                    if name == "early":
                        early[k].start()
                    if name == "late":
                        late[k].start()
                    if name == "onward":
                        early[k].wait_recv()
                        onward[k].start()

    due("start")

    p_steps, p_sent = all_reduce(
        p_part, p_core, p1x, p1y, p2x, p2y, p_zh, p_z, p_full, p_send, p_recv, place, 1.0 / 32, False
    )
    q_steps, q_sent = all_reduce(
        q_part, q_core, q1x, q1y, q2x, q2y, q_zh, q_z, q_full, q_send, q_recv, place, 1.0 / 32, True
    )

    with jax.named_scope("left_terms"):
        xt[pl.ds(ROWS, P_ROWS - ROWS)] = jnp.zeros((P_ROWS - ROWS, TOKENS), BF16)
        loads[1].wait()
        loads[0].wait()
        own = pl.ds(pl.multiple_of(z * TOKENS, TOKENS), TOKENS)
        mine = pl.ds(pl.multiple_of(z * MY_ROWS, 8), MY_ROWS)
        t_cat[...] = jnp.concatenate(
            split(
                dot(g_all[own, 0 : COLS // 2], q_in[0 : COLS // 2, :])
                + dot(g_all[own, COLS // 2 : COLS], q_in[COLS // 2 : COLS, :])
            ),
            axis=1,
        )
        loads[2].wait()
        both = dot(xt[...], t_cat[...])
        p_flat[...] = both[:, 0:RANK] + both[:, RANK : 2 * RANK]
        loads[3].wait()
        p_flat[mine, :] += dot(e_buf[:, 0 : COLS // 2], q_in[0 : COLS // 2, :]) + dot(
            e_buf[:, COLS // 2 : COLS], q_in[COLS // 2 : COLS, :]
        )
        p_part[...] = p_flat[...].reshape(p_part.shape)

    with jax.named_scope("left_reduce"):
        for k, step in enumerate(p_steps):
            due("p%d" % k)
            step()

    with jax.named_scope("factor"):
        p_flat[...] = p_full[...].reshape(P_ROWS, RANK)
        mat[:, 0:RANK] = dot(p_flat[...], p_flat[...], 0, 0, HIGHEST)
        diagonal = lax.broadcasted_iota(jnp.int32, (RANK, RANK), 0) == lax.broadcasted_iota(
            jnp.int32, (RANK, RANK), 1
        )
        mat[:, RANK : 2 * RANK] = jnp.where(diagonal, 1.0, 0.0)
    with jax.named_scope("cholesky"):
        cholesky_inverse(mat)

    with jax.named_scope("right_terms"):
        inverse = mat[:, RANK : 2 * RANK]
        p_rows[0:RANK, :], p_rows[RANK : 2 * RANK, :] = split(dot(inverse, p_flat[...], 1, 1, HIGHEST))
        y_sum = dot(p_rows[...], xt[...])
        y_cat[0:RANK, :], y_cat[RANK : 2 * RANK, :] = split(y_sum[0:RANK] + y_sum[RANK : 2 * RANK])
        p_mine = p_flat[mine, :]
        p_t[0:RANK, :], p_t[RANK : 2 * RANK, :] = split(dot(inverse, p_mine, 1, 1, HIGHEST))
        m_high, m_low = split(dot(p_mine, inverse, 1, 1, HIGHEST))
        p_cat[:, 0:RANK] = m_high
        p_cat[:, RANK : 2 * RANK] = m_low
        p_cat[:, 2 * RANK : 3 * RANK] = m_high

        q_part[1, 3, 3] = jnp.zeros((RANK, CHUNK), F32)

        def right_terms(which):
            def chunk(i, carry):
                s = NC * i + which
                cols = pl.ds(pl.multiple_of(s * CHUNK, CHUNK), CHUNK)
                both = dot(y_cat[...], g_all[own, cols]) + dot(p_t[...], e_buf[:, cols])
                q_part[slot(s)] = both[0:RANK] + both[RANK : 2 * RANK]
                return carry

            lax.fori_loop(0, 16 - which, chunk, 0)

        right_terms(1 - core)
        due("q0")
        q_steps[0]()
        right_terms(core)

    for k, step in enumerate(q_steps[1:-1], 1):
        due("q%d" % k)
        step()

    loads[4].wait()
    for copy in x_copies:
        copy.wait_recv()

    def wait_piece(i):
        for copy in late[2 * i : 2 * i + 2] + onward[2 * i : 2 * i + 2]:
            copy.wait_recv()

    def error_chunk(s, carry):
        cols = pl.ds(pl.multiple_of(s * CHUNK, CHUNK), CHUNK)
        e_buf[:, cols] = error_block(xr, g_all, e_buf, p_cat, cols, stacked(q_full[slot(s)]))
        return carry

    with jax.named_scope("error_next"):
        wait_piece(0)
        wait_piece(1)
        ahead = PIECES[1][1] // NC
        lax.fori_loop(0, ahead, lambda i, carry: error_chunk(NC * i + core, carry), 0)
        q_steps[-1]()
        lax.fori_loop(0, ahead, lambda i, carry: error_chunk(NC * i + 1 - core, carry), 0)
        for i in range(2, N_PIECE - 3):
            wait_piece(i)
            lax.fori_loop(*PIECES[i], error_chunk, 0)

    with jax.named_scope("right_factor"):
        first_line = (31 * z) // 4

        def lines(i, carry):
            s = first_line + i
            q_lines[pl.ds(pl.multiple_of(i * CHUNK, CHUNK), CHUNK), :] = q_full[slot(s)].T
            return carry

        lax.fori_loop(0, 9, lines, 0)
        offset = (CHUNK - 64 * z) % CHUNK
        qf_store = pltpu.make_async_copy(q_lines.at[pl.ds(offset, ROWS)], qf_out, store.at[0])
        qf_store.start()
        for s in range(TAIL, CHUNKS):
            q_tail[s - TAIL] = stacked(q_full[slot(s)])

    with jax.named_scope("error_next_end"):
        wait_piece(N_PIECE - 3)
        lax.fori_loop(*PIECES[N_PIECE - 3], error_chunk, 0)
        p_sent()
        q_sent()
        for copy in x_copies + early + late + onward[:-4]:
            copy.wait_send()
        qf_store.wait()

    with jax.named_scope("finish"):
        wait_piece(N_PIECE - 2)
        wait_piece(N_PIECE - 1)
        for copy in onward[-4:]:
            copy.wait_send()


def closing(qf_in, e_buf, xr, g_all, p_cat, q_tail, qf_out, err_out, tail, done):
    copies = [pltpu.make_async_copy(qf_in, qf_out, done.at[0])]
    for k in range(4):
        cols = pl.ds(k * TAIL // 4 * CHUNK, TAIL // 4 * CHUNK)
        copies.append(pltpu.make_async_copy(e_buf.at[:, cols], err_out.at[0, :, cols], done.at[1 + k]))
    for copy in copies:
        copy.start()
    for i in range(CHUNKS - TAIL):
        cols = pl.ds((TAIL + i) * CHUNK, CHUNK)
        tail[i] = error_block(xr, g_all, e_buf, p_cat, cols, q_tail[i])
        copies.append(pltpu.make_async_copy(tail.at[i], err_out.at[0, :, cols], done.at[5 + i]))
        copies[-1].start()
    for copy in copies:
        copy.wait()


def per_device(inputs, out_grads, error_buf, q_prev):
    any_space = pl.BlockSpec(memory_space=pl.ANY)
    vmem = pl.BlockSpec(memory_space=pltpu.VMEM)

    def reduce_scratch(height, width):
        stage = pltpu.VMEM((3, 4, height // 2, width), F32)
        small = pltpu.VMEM((3, height // 2, width), F32)
        return [
            pltpu.VMEM((NC, NX, NY, height, width), F32),
            pltpu.VMEM((NX, NY, height, width), F32),
            stage, stage, small, small,
            pltpu.VMEM((2, height // NZ // 2, width), F32),
            pltpu.VMEM((3, height // NZ, width), F32),
            pltpu.VMEM((NC, NX, NY, height, width), F32),
        ]

    dma = pltpu.SemaphoreType.DMA
    held = pl.pallas_call(
        kernel,
        out_shape=(
            pltpu.VMEM((ROWS, RANK), F32),
            pltpu.VMEM((MY_ROWS, COLS), BF16),
            pltpu.VMEM((MY_ROWS, NZ * TOKENS), BF16),
            pltpu.VMEM((NZ * TOKENS, COLS), BF16),
            pltpu.VMEM((MY_ROWS, 3 * RANK), BF16),
            pltpu.VMEM((CHUNKS - TAIL, 3 * RANK, CHUNK), BF16),
        ),
        in_specs=[any_space] * 4,
        out_specs=(vmem,) * 6,
        scratch_shapes=[
            pltpu.VMEM((P_ROWS, TOKENS), BF16),
            pltpu.VMEM((COLS, RANK), BF16),
            pltpu.VMEM((P_ROWS, RANK), F32),
            pltpu.VMEM((TOKENS, 2 * RANK), BF16),
            pltpu.VMEM((RANK, 2 * RANK), F32),
            pltpu.VMEM((2 * RANK, P_ROWS), BF16),
            pltpu.VMEM((2 * RANK, MY_ROWS), BF16),
            pltpu.VMEM((2 * RANK, TOKENS), BF16),
            pltpu.VMEM((9 * CHUNK, RANK), F32),
            *reduce_scratch(P_SLICE, RANK),
            *reduce_scratch(RANK, CHUNK),
            dma((5,)), dma((1,)),
            dma((N_COPY,)), dma((N_COPY,)), dma((N_COPY,)), dma((N_COPY,)),
            dma((4,)), dma((4,)), dma((6, N_PIECE)), dma((6, N_PIECE)),
        ],
        compiler_params=pltpu.CompilerParams(
            collective_id=0, has_side_effects=True, vmem_limit_bytes=32 * 1024 * 1024
        ),
    )(inputs[0].T, out_grads[0], error_buf[0], q_prev)
    return pl.pallas_call(
        closing,
        out_shape=(
            jax.ShapeDtypeStruct((ROWS, RANK), F32),
            jax.ShapeDtypeStruct((1, MY_ROWS, COLS), BF16),
        ),
        in_specs=[vmem] * 6,
        out_specs=(any_space, any_space),
        scratch_shapes=[
            pltpu.VMEM((CHUNKS - TAIL, MY_ROWS, CHUNK), BF16),
            dma((5 + CHUNKS - TAIL,)),
        ],
        compiler_params=pltpu.CompilerParams(vmem_limit_bytes=6 * 1024 * 1024),
    )(*(pltpu.with_memory_space_constraint(v, pltpu.VMEM) for v in held))


def solution(mesh):
    in_specs = (
        P("machine", "local", None),
        P("machine", "local", None),
        P("machine", "local", None),
        P(),
    )
    out_specs = (P("local", None), P("machine", "local", None))
    return jax.shard_map(
        per_device, mesh=mesh, in_specs=in_specs, out_specs=out_specs, check_vma=False
    )
```

```python
import jax
import jax.numpy as jnp
from jax import lax
from jax.experimental import pallas as pl
from jax.experimental.pallas import tpu as pltpu
from jax.sharding import PartitionSpec as P

MESH = pl.DeviceIdType.MESH
F32, BF16 = jnp.float32, jnp.bfloat16
HIGHEST = lax.Precision.HIGHEST

NX, NY, NC, NZ = 4, 4, 2, 4
TOKENS, ROWS, COLS, RANK = 256, 1984, 7936, 128
MY_ROWS = ROWS // NZ
HALF = TOKENS // 2
CHUNK = 256
CHUNKS = COLS // CHUNK
P_ROWS = 2048
P_SLICE = P_ROWS // 32
PIECES = ((0, 5), (5, 10), (10, 15), (15, 20), (20, 24), (24, 28), (28, 30), (30, 31))
N_PIECE = len(PIECES)
TAIL = 28
N_COPY = 34
PANEL = 32
PLAN = {
    "start": (("early", 0, 2), ("x", 0, 3)),
    "p4": (("early", 2, 3),),
    "p5": (("early", 3, 8), ("late", 0, 4)),
    "q4": (("late", 4, 5),),
    "q5": (("late", 5, 6),),
    "q6": (("late", 6, 8),),
    "q7": (("onward", 0, 8),),
}


def dot(a, b, lhs=1, rhs=0, precision=None):
    return lax.dot_general(
        a, b, (((lhs,), (rhs,)), ((), ())), precision=precision, preferred_element_type=F32
    )


def split(value):
    high = value.astype(BF16)
    return high, (value - high.astype(F32)).astype(BF16)


def slot(s):
    return s % NC, s // (NC * NY), s // NC % NY


def stacked(q_block):
    high, low = split(q_block)
    return jnp.concatenate([high, high, low], axis=0)


def error_block(xr, g_all, e_buf, p_cat, cols, q_cat):
    merged = dot(xr[...], g_all[:, cols]) + e_buf[:, cols].astype(F32)
    return (merged - dot(p_cat[...], q_cat)).astype(BF16)


def all_reduce(part, from_core, r1x, r1y, r2x, r2y, rz_half, rz, full, send, recv, place, scale, relayed):
    x, y, core, z = place
    height = part.shape[3]
    upper, lower = pl.ds(0, height // 2), pl.ds(height // 2, height // 2)
    running = {}

    up, across_z, down = (z + 1) % NZ, (z + 2) % NZ, (z + 3) % NZ

    def quarter(k):
        return pl.ds(pl.multiple_of(k * (height // NZ), 8), height // NZ)

    def half(k, which):
        size = height // NZ // 2
        return pl.ds(pl.multiple_of(k * 2 * size + which * size, 8), size)

    def start(key, number, src, dst, where):
        px, py, pcore, pz = where
        copy = pltpu.make_async_remote_copy(
            src_ref=src, dst_ref=dst, send_sem=send.at[number], recv_sem=recv.at[number],
            device_id={"machine": (px * NY + py) * NC + pcore, "local": pz}, device_id_type=MESH,
        )
        copy.start()
        running.setdefault(key, []).append(copy)

    def arrive(key):
        for copy in running[key]:
            copy.wait_recv()

    def begin():
        start("core", 0, part.at[1 - core], from_core, (x, y, 1 - core, z))

    def first():
        arrive("core")

        def add(s, carry):
            a, b = s // NY, s % NY
            part[core, a, b] = part[core, a, b] + from_core[a, b]
            return carry

        lax.fori_loop(0, NX * NY, add, 0)
        for d in range(1, 4):
            px, py = (x + d) % NX, (y + d) % NY
            start("1x", 0 + d, part.at[core, px, :, upper], r1x.at[d - 1], (px, y, core, z))
            start("1y", 3 + d, part.at[core, :, py, lower], r1y.at[d - 1], (x, py, core, z))

    def second():
        arrive("1x")
        arrive("1y")
        for b in range(NY):
            part[core, x, b, upper] = part[core, x, b, upper] + r1x[0, b] + r1x[1, b] + r1x[2, b]
        for a in range(NX):
            part[core, a, y, lower] = part[core, a, y, lower] + r1y[0, a] + r1y[1, a] + r1y[2, a]
        for d in range(1, 4):
            px, py = (x + d) % NX, (y + d) % NY
            start("2y", 6 + d, part.at[core, x, py, upper], r2y.at[d - 1], (x, py, core, z))
            start("2x", 9 + d, part.at[core, px, y, lower], r2x.at[d - 1], (px, y, core, z))

    def across():
        arrive("2x")
        arrive("2y")
        part[core, x, y, upper] = part[core, x, y, upper] + r2y[0] + r2y[1] + r2y[2]
        part[core, x, y, lower] = part[core, x, y, lower] + r2x[0] + r2x[1] + r2x[2]
        mine = part.at[core, x, y]
        if not relayed:
            for d in range(1, 4):
                to = (z + d) % NZ
                start("zb", 12 + d, mine.at[quarter(to)], rz.at[d - 1], (x, y, core, to))
            return
        start("za", 13, mine.at[half(across_z, 0)], rz_half.at[0], (x, y, core, up))
        start("za", 14, mine.at[half(across_z, 1)], rz_half.at[1], (x, y, core, down))

    def relay():
        arrive("za")
        part[core, x, y, half(up, 0)] = part[core, x, y, half(up, 0)] + rz_half[0]
        part[core, x, y, half(down, 1)] = part[core, x, y, half(down, 1)] + rz_half[1]
        mine = part.at[core, x, y]
        start("zb", 15, mine.at[quarter(up)], rz.at[0], (x, y, core, up))
        start("zb", 29, mine.at[quarter(down)], rz.at[1], (x, y, core, down))

    def total():
        arrive("zb")
        mine = quarter(z)
        others = rz[0] + rz[1] if relayed else rz[0] + rz[1] + rz[2]
        full[core, x, y, mine] = (part[core, x, y, mine] + others) * scale
        mine = full.at[core, x, y, quarter(z)]
        if not relayed:
            for d in range(1, 4):
                start("zd", 28 + d, mine, mine, (x, y, core, (z + d) % NZ))
            return
        start("zc", 30, mine, mine, (x, y, core, up))
        start("zc", 31, mine, mine, (x, y, core, down))

    def onward():
        arrive("zc")
        mine = full.at[core, x, y, half(down, 0)]
        start("zd", 32, mine, mine, (x, y, core, up))
        mine = full.at[core, x, y, half(up, 1)]
        start("zd", 33, mine, mine, (x, y, core, down))

    def joined():
        arrive("zd")
        for d in range(1, 4):
            px, py = (x + d) % NX, (y + d) % NY
            mine = full.at[core, x, y, upper]
            start("3y", 15 + d, mine, mine, (x, py, core, z))
            mine = full.at[core, x, y, lower]
            start("3x", 18 + d, mine, mine, (px, y, core, z))

    def spread():
        arrive("3x")
        arrive("3y")
        for d in range(1, 4):
            px, py = (x + d) % NX, (y + d) % NY
            mine = full.at[core, x, :, upper]
            start("4x", 21 + d, mine, mine, (px, y, core, z))
            mine = full.at[core, :, y, lower]
            start("4y", 24 + d, mine, mine, (x, py, core, z))

    def share():
        arrive("4x")
        arrive("4y")
        start("share", 28, full.at[core], full.at[core], (x, y, 1 - core, z))

    def end():
        arrive("share")

    def sent():
        for copies in running.values():
            for copy in copies:
                copy.wait_send()

    if relayed:
        return [begin, first, second, across, relay, total, onward, joined, spread, share, end], sent
    return [begin, first, second, across, total, joined, spread, share, end], sent


def cholesky_inverse(mat):
    shape = (PANEL, RANK)
    lane = lax.broadcasted_iota(jnp.int32, shape, 1)
    sub = lax.broadcasted_iota(jnp.int32, shape, 0)

    def panel(b, carry):
        rows = pl.ds(pl.multiple_of(b * PANEL, PANEL), PANEL)
        left = pltpu.roll(mat[rows, 0:RANK], (RANK - b * PANEL) % RANK, 1)
        right = mat[rows, RANK : 2 * RANK]
        pivots = jnp.ones(shape, F32)
        for first in range(0, PANEL, 8):
            columns = [jnp.broadcast_to(left[:, first + k : first + k + 1], shape) for k in range(8)]
            for k in range(8):
                j = first + k
                pivot = jnp.broadcast_to(columns[k][j : j + 1, :], shape)
                factor = jnp.where(sub > j, columns[k] * (1.0 / pivot), 0.0)
                for n in range(k + 1, 8):
                    columns[n] = columns[n] - factor * columns[n][j : j + 1, :]
                left = left - factor * left[j : j + 1, :]
                right = right - factor * right[j : j + 1, :]
                pivots = jnp.where(sub == j, pivot, pivots)
        scale = lax.rsqrt(pivots)
        scale = scale * (1.5 - 0.5 * pivots * scale * scale)
        left = pltpu.roll(left * scale, b * PANEL, 1)
        right = right * scale
        mat[rows, 0:RANK] = left
        mat[rows, RANK : 2 * RANK] = right
        below = jnp.where(lane >= (b + 1) * PANEL, left, 0.0)
        both = jnp.concatenate([left, right], axis=1)
        mat[...] = mat[...] - dot(below, both, 0, 0, HIGHEST)
        return carry

    lax.fori_loop(0, RANK // PANEL, panel, 0)


def kernel(
    xt_hbm, g_hbm, e_hbm, q_hbm, qf_out, e_buf, xr, g_all, p_cat, q_tail,
    xt, q_in, p_flat, t_cat, mat, p_rows, p_t, y_cat, q_lines,
    p_part, p_core, p1x, p1y, p2x, p2y, p_zh, p_z, p_full,
    q_part, q_core, q1x, q1y, q2x, q2y, q_zh, q_z, q_full,
    load, store, p_send, p_recv, q_send, q_recv, x_send, x_recv, g_send, g_recv,
):
    m, z = lax.axis_index("machine"), lax.axis_index("local")
    core, y, x = m % NC, (m // NC) % NY, m // (NC * NY)
    place = (x, y, core, z)
    left, right = (z + NZ - 1) % NZ, (z + 1) % NZ

    with jax.named_scope("barrier"):
        barrier = pltpu.get_barrier_semaphore()
        for d in range(1, 4):
            for px, py, pcore, pz in (
                (x, y, core, (z + d) % NZ), ((x + d) % NX, y, core, z), (x, (y + d) % NY, core, z)
            ):
                pl.semaphore_signal(
                    barrier, inc=1, device_id_type=MESH,
                    device_id={"machine": (px * NY + py) * NC + pcore, "local": pz},
                )
        pl.semaphore_signal(
            barrier, inc=1, device_id_type=MESH,
            device_id={"machine": (x * NY + y) * NC + 1 - core, "local": z},
        )

    loads = [
        pltpu.make_async_copy(g_hbm, g_all.at[pl.ds(z * TOKENS, TOKENS)], load.at[0]),
        pltpu.make_async_copy(q_hbm, q_in, load.at[1]),
        pltpu.make_async_copy(xt_hbm, xt.at[pl.ds(0, ROWS)], load.at[2]),
        pltpu.make_async_copy(e_hbm, e_buf, load.at[3]),
        pltpu.make_async_copy(
            xt_hbm.at[pl.ds(z * MY_ROWS, MY_ROWS)], xr.at[:, pl.ds(z * TOKENS, TOKENS)], load.at[4]
        ),
    ]
    for copy in loads:
        copy.start()

    pl.semaphore_wait(barrier, 10)

    x_copies = []
    for d in range(1, 4):
        pz = (z + d) % NZ
        x_copies.append(pltpu.make_async_remote_copy(
            src_ref=xt_hbm.at[pl.ds(pz * MY_ROWS, MY_ROWS)],
            dst_ref=xr.at[:, pl.ds(z * TOKENS, TOKENS)],
            send_sem=x_send.at[d], recv_sem=x_recv.at[d],
            device_id={"machine": m, "local": pz}, device_id_type=MESH,
        ))

    def g_copy(src, dst, kind, piece, half, owner, target):
        first, last = PIECES[piece]
        rows = pl.ds(owner * TOKENS + half * HALF, HALF)
        cols = pl.ds(first * CHUNK, (last - first) * CHUNK)
        dst = dst.at[rows, cols]
        src = dst if src is None else src.at[pl.ds(half * HALF, HALF), cols]
        return pltpu.make_async_remote_copy(
            src_ref=src, dst_ref=dst, send_sem=g_send.at[kind, piece], recv_sem=g_recv.at[kind, piece],
            device_id={"machine": m, "local": target}, device_id_type=MESH,
        )

    early, late, onward = [], [], []
    for i in range(N_PIECE):
        early += [g_copy(g_hbm, g_all, 0, i, 0, z, right), g_copy(g_hbm, g_all, 1, i, 1, z, left)]
        late += [g_copy(g_hbm, g_all, 2, i, 1, z, right), g_copy(g_hbm, g_all, 3, i, 0, z, left)]
        onward += [g_copy(None, g_all, 4, i, 0, left, right), g_copy(None, g_all, 5, i, 1, right, left)]
    def due(point):
        for name, first, last in PLAN.get(point, ()):
            for i in range(first, last):
                if name == "x":
                    x_copies[i].start()
                for k in (2 * i, 2 * i + 1):
                    if name == "early":
                        early[k].start()
                    if name == "late":
                        late[k].start()
                    if name == "onward":
                        early[k].wait_recv()
                        onward[k].start()

    due("start")

    p_steps, p_sent = all_reduce(
        p_part, p_core, p1x, p1y, p2x, p2y, p_zh, p_z, p_full, p_send, p_recv, place, 1.0 / 32, False
    )
    q_steps, q_sent = all_reduce(
        q_part, q_core, q1x, q1y, q2x, q2y, q_zh, q_z, q_full, q_send, q_recv, place, 1.0 / 32, True
    )

    with jax.named_scope("left_terms"):
        xt[pl.ds(ROWS, P_ROWS - ROWS)] = jnp.zeros((P_ROWS - ROWS, TOKENS), BF16)
        loads[1].wait()
        loads[0].wait()
        own = pl.ds(pl.multiple_of(z * TOKENS, TOKENS), TOKENS)
        mine = pl.ds(pl.multiple_of(z * MY_ROWS, 8), MY_ROWS)
        t_cat[...] = jnp.concatenate(
            split(
                dot(g_all[own, 0 : COLS // 2], q_in[0 : COLS // 2, :])
                + dot(g_all[own, COLS // 2 : COLS], q_in[COLS // 2 : COLS, :])
            ),
            axis=1,
        )
        loads[2].wait()
        both = dot(xt[...], t_cat[...])
        p_flat[...] = both[:, 0:RANK] + both[:, RANK : 2 * RANK]
        loads[3].wait()
        p_flat[mine, :] += dot(e_buf[:, 0 : COLS // 2], q_in[0 : COLS // 2, :]) + dot(
            e_buf[:, COLS // 2 : COLS], q_in[COLS // 2 : COLS, :]
        )
        p_part[...] = p_flat[...].reshape(p_part.shape)

    with jax.named_scope("left_reduce"):
        for k, step in enumerate(p_steps):
            due("p%d" % k)
            step()

    with jax.named_scope("factor"):
        p_flat[...] = p_full[...].reshape(P_ROWS, RANK)
        mat[:, 0:RANK] = dot(p_flat[...], p_flat[...], 0, 0, HIGHEST)
        diagonal = lax.broadcasted_iota(jnp.int32, (RANK, RANK), 0) == lax.broadcasted_iota(
            jnp.int32, (RANK, RANK), 1
        )
        mat[:, RANK : 2 * RANK] = jnp.where(diagonal, 1.0, 0.0)
    with jax.named_scope("cholesky"):
        cholesky_inverse(mat)

    with jax.named_scope("right_terms"):
        inverse = mat[:, RANK : 2 * RANK]
        p_rows[0:RANK, :], p_rows[RANK : 2 * RANK, :] = split(dot(inverse, p_flat[...], 1, 1, HIGHEST))
        y_sum = dot(p_rows[...], xt[...])
        y_cat[0:RANK, :], y_cat[RANK : 2 * RANK, :] = split(y_sum[0:RANK] + y_sum[RANK : 2 * RANK])
        p_mine = p_flat[mine, :]
        p_t[0:RANK, :], p_t[RANK : 2 * RANK, :] = split(dot(inverse, p_mine, 1, 1, HIGHEST))
        m_high, m_low = split(dot(p_mine, inverse, 1, 1, HIGHEST))
        p_cat[:, 0:RANK] = m_high
        p_cat[:, RANK : 2 * RANK] = m_low
        p_cat[:, 2 * RANK : 3 * RANK] = m_high

        q_part[1, 3, 3] = jnp.zeros((RANK, CHUNK), F32)

        def right_terms(which):
            def chunk(i, carry):
                s = NC * i + which
                cols = pl.ds(pl.multiple_of(s * CHUNK, CHUNK), CHUNK)
                both = dot(y_cat[...], g_all[own, cols]) + dot(p_t[...], e_buf[:, cols])
                q_part[slot(s)] = both[0:RANK] + both[RANK : 2 * RANK]
                return carry

            lax.fori_loop(0, 16 - which, chunk, 0)

        right_terms(1 - core)
        due("q0")
        q_steps[0]()
        right_terms(core)

    for k, step in enumerate(q_steps[1:-1], 1):
        due("q%d" % k)
        step()

    loads[4].wait()
    for copy in x_copies:
        copy.wait_recv()

    def wait_piece(i):
        for copy in late[2 * i : 2 * i + 2] + onward[2 * i : 2 * i + 2]:
            copy.wait_recv()

    def error_chunk(s, carry):
        cols = pl.ds(pl.multiple_of(s * CHUNK, CHUNK), CHUNK)
        e_buf[:, cols] = error_block(xr, g_all, e_buf, p_cat, cols, stacked(q_full[slot(s)]))
        return carry

    with jax.named_scope("error_next"):
        wait_piece(0)
        wait_piece(1)
        ahead = PIECES[1][1] // NC
        lax.fori_loop(0, ahead, lambda i, carry: error_chunk(NC * i + core, carry), 0)
        q_steps[-1]()
        lax.fori_loop(0, ahead, lambda i, carry: error_chunk(NC * i + 1 - core, carry), 0)
        for i in range(2, N_PIECE - 3):
            wait_piece(i)
            lax.fori_loop(*PIECES[i], error_chunk, 0)

    with jax.named_scope("right_factor"):
        first_line = (31 * z) // 4

        def lines(i, carry):
            s = first_line + i
            q_lines[pl.ds(pl.multiple_of(i * CHUNK, CHUNK), CHUNK), :] = q_full[slot(s)].T
            return carry

        lax.fori_loop(0, 9, lines, 0)
        offset = (CHUNK - 64 * z) % CHUNK
        qf_store = pltpu.make_async_copy(q_lines.at[pl.ds(offset, ROWS)], qf_out, store.at[0])
        qf_store.start()
        for s in range(TAIL, CHUNKS):
            q_tail[s - TAIL] = stacked(q_full[slot(s)])

    with jax.named_scope("error_next_end"):
        wait_piece(N_PIECE - 3)
        lax.fori_loop(*PIECES[N_PIECE - 3], error_chunk, 0)
        p_sent()
        q_sent()
        for copy in x_copies + early + late + onward[:-4]:
            copy.wait_send()
        qf_store.wait()

    with jax.named_scope("finish"):
        wait_piece(N_PIECE - 2)
        wait_piece(N_PIECE - 1)
        for copy in onward[-4:]:
            copy.wait_send()


def closing(qf_in, e_buf, xr, g_all, p_cat, q_tail, qf_out, err_out, tail, done):
    copies = [pltpu.make_async_copy(qf_in, qf_out, done.at[0])]
    for k in range(4):
        cols = pl.ds(k * TAIL // 4 * CHUNK, TAIL // 4 * CHUNK)
        copies.append(pltpu.make_async_copy(e_buf.at[:, cols], err_out.at[0, :, cols], done.at[1 + k]))
    for copy in copies:
        copy.start()
    for i in range(CHUNKS - TAIL):
        cols = pl.ds((TAIL + i) * CHUNK, CHUNK)
        tail[i] = error_block(xr, g_all, e_buf, p_cat, cols, q_tail[i])
        copies.append(pltpu.make_async_copy(tail.at[i], err_out.at[0, :, cols], done.at[5 + i]))
        copies[-1].start()
    for copy in copies:
        copy.wait()


def per_device(inputs, out_grads, error_buf, q_prev):
    any_space = pl.BlockSpec(memory_space=pl.ANY)
    vmem = pl.BlockSpec(memory_space=pltpu.VMEM)

    def reduce_scratch(height, width):
        stage = pltpu.VMEM((3, 4, height // 2, width), F32)
        small = pltpu.VMEM((3, height // 2, width), F32)
        return [
            pltpu.VMEM((NC, NX, NY, height, width), F32),
            pltpu.VMEM((NX, NY, height, width), F32),
            stage, stage, small, small,
            pltpu.VMEM((2, height // NZ // 2, width), F32),
            pltpu.VMEM((3, height // NZ, width), F32),
            pltpu.VMEM((NC, NX, NY, height, width), F32),
        ]

    dma = pltpu.SemaphoreType.DMA
    held = pl.pallas_call(
        kernel,
        out_shape=(
            pltpu.VMEM((ROWS, RANK), F32),
            pltpu.VMEM((MY_ROWS, COLS), BF16),
            pltpu.VMEM((MY_ROWS, NZ * TOKENS), BF16),
            pltpu.VMEM((NZ * TOKENS, COLS), BF16),
            pltpu.VMEM((MY_ROWS, 3 * RANK), BF16),
            pltpu.VMEM((CHUNKS - TAIL, 3 * RANK, CHUNK), BF16),
        ),
        in_specs=[any_space] * 4,
        out_specs=(vmem,) * 6,
        scratch_shapes=[
            pltpu.VMEM((P_ROWS, TOKENS), BF16),
            pltpu.VMEM((COLS, RANK), BF16),
            pltpu.VMEM((P_ROWS, RANK), F32),
            pltpu.VMEM((TOKENS, 2 * RANK), BF16),
            pltpu.VMEM((RANK, 2 * RANK), F32),
            pltpu.VMEM((2 * RANK, P_ROWS), BF16),
            pltpu.VMEM((2 * RANK, MY_ROWS), BF16),
            pltpu.VMEM((2 * RANK, TOKENS), BF16),
            pltpu.VMEM((9 * CHUNK, RANK), F32),
            *reduce_scratch(P_SLICE, RANK),
            *reduce_scratch(RANK, CHUNK),
            dma((5,)), dma((1,)),
            dma((N_COPY,)), dma((N_COPY,)), dma((N_COPY,)), dma((N_COPY,)),
            dma((4,)), dma((4,)), dma((6, N_PIECE)), dma((6, N_PIECE)),
        ],
        compiler_params=pltpu.CompilerParams(
            collective_id=0, has_side_effects=True, vmem_limit_bytes=32 * 1024 * 1024
        ),
    )(inputs[0].T, out_grads[0], error_buf[0], q_prev)
    return pl.pallas_call(
        closing,
        out_shape=(
            jax.ShapeDtypeStruct((ROWS, RANK), F32),
            jax.ShapeDtypeStruct((1, MY_ROWS, COLS), BF16),
        ),
        in_specs=[vmem] * 6,
        out_specs=(any_space, any_space),
        scratch_shapes=[
            pltpu.VMEM((CHUNKS - TAIL, MY_ROWS, CHUNK), BF16),
            dma((5 + CHUNKS - TAIL,)),
        ],
        compiler_params=pltpu.CompilerParams(vmem_limit_bytes=6 * 1024 * 1024),
    )(*(pltpu.with_memory_space_constraint(v, pltpu.VMEM) for v in held))


def solution(mesh):
    in_specs = (
        P("machine", "local", None),
        P("machine", "local", None),
        P("machine", "local", None),
        P(),
    )
    out_specs = (P("local", None), P("machine", "local", None))
    return jax.shard_map(
        per_device, mesh=mesh, in_specs=in_specs, out_specs=out_specs, check_vma=False
    )
```
